256 devices in a mesh: inline: 8 (over z_hi, core), tile: 32 (over z_lo, y, x).
Axes of the slice: x: 4, y: 4, z: 8 (z_hi: 4, z_lo: 2; z = z_hi * 2 + z_lo), core: 2. Of those that a mesh axis runs over, the one named last changes fastest.
Arguments:
- features: bfloat16 [96, 16, 64, 128], P(None, 'inline', 'tile'), may hold values from -13 to 13
- conv1_weight: bfloat16 [96, 27, 96], replicated, may hold values from -0.125 to 0.125
- conv2_weight: bfloat16 [96, 27, 96], replicated, may hold values from -0.125 to 0.125
- fault_head: bfloat16 [96, 2], replicated, may hold values from -0.625 to 0.625
- horizon_head: bfloat16 [96, 4], replicated, may hold values from -0.625 to 0.625
- salt_query: bfloat16 [96], replicated, may hold values from -0.625 to 0.625
- salt_head: bfloat16 [96, 2], replicated, may hold values from -0.625 to 0.625
- fault_labels: int32 [16, 64, 128], P('inline', 'tile'), may hold values from 0 to 1
- horizon_labels: int32 [16, 64, 128], P('inline', 'tile'), may hold values from 0 to 3
- salt_labels: int32 [16, 128], P('inline'), may hold values from 0 to 1
Outputs:
- grads: float32 [2, 3, 248832], P(None, None, ('inline', 'tile'))
- gram: float32 [2, 3, 3], replicated
The draws below stay inside these ranges and needn't reach their ends.
All inputs are finite; a program needn't handle non-finite values.
Results may differ from the reference program's by a relative error of at most 0.0043.
Values may be sent and summed in bfloat16 or wider, within the bound.
A program may use at most 128 MiB of HBM per device.

```python
import math
import jax
import jax.numpy as jnp
from jax import lax

C = 96
FAULT_CLASSES = 2
HORIZON_CLASSES = 4
SALT_CLASSES = 2
D1 = 1
D2 = 2
Y = 128
NX = 16
NZ = 64


def draw_features(key, part):
    chan = 10.0 ** (jnp.arange(C, dtype=jnp.float32) / (C - 1) - 0.5)
    base = jnp.clip(jax.random.normal(key, (C, NX, NZ, Y), jnp.float32), -4.0, 4.0)
    return (base * chan[:, None, None, None]).astype(jnp.bfloat16)


def plant(entries, own_key, smallest, top_value):
    shape = entries.shape
    place = [jax.random.randint(jax.random.fold_in(own_key, axis), (), 0, shape[axis]) for axis in range(len(shape))]
    entries = entries.at[tuple(place)].set(smallest)
    longest = shape.index(max(shape))
    place[longest] = (place[longest] + 1) % shape[longest]
    return entries.at[tuple(place)].set(top_value)


def centred(rng, extent, deviation, reach, kind=jnp.bfloat16):
    return jnp.clip(deviation * jax.random.normal(rng, extent, jnp.float32), -reach, reach).astype(kind)


def setup_inputs(seed: int = 0) -> dict:
    keys = jax.random.split(jax.random.key(seed), 11)
    return {
        "features": draw_features(jax.random.fold_in(keys[10], 71), 0),
        "conv1_weight": centred(keys[1], (C, 27, C), (27 * C) ** -0.5, 0.125),
        "conv2_weight": centred(keys[2], (C, 27, C), (27 * C) ** -0.5, 0.125),
        "fault_head": centred(keys[3], (C, FAULT_CLASSES), C ** -0.5, 0.625),
        "horizon_head": centred(keys[4], (C, HORIZON_CLASSES), C ** -0.5, 0.625),
        "salt_query": centred(keys[5], (C,), C ** -0.5, 0.625),
        "salt_head": centred(keys[6], (C, SALT_CLASSES), C ** -0.5, 0.625),
        "fault_labels": plant(jax.random.randint(keys[7], (NX, NZ, Y), 0, FAULT_CLASSES), jax.random.fold_in(keys[7], 1), 0, FAULT_CLASSES - 1).astype(jnp.int32),
        "horizon_labels": plant(jax.random.randint(keys[8], (NX, NZ, Y), 0, HORIZON_CLASSES), jax.random.fold_in(keys[8], 1), 0, HORIZON_CLASSES - 1).astype(jnp.int32),
        "salt_labels": plant(jax.random.randint(keys[9], (NX, Y), 0, SALT_CLASSES), jax.random.fold_in(keys[9], 1), 0, SALT_CLASSES - 1).astype(jnp.int32),
    }


CAPPING = 8.0
HIGH = lax.Precision.HIGHEST

def capped(value):
    return CAPPING * jnp.tanh(value / CAPPING)

def cap_slope(value):
    squash = jnp.tanh(value / CAPPING)
    return 1.0 - squash * squash

def silu_slope(value):
    sig = jax.nn.sigmoid(value)
    return sig * (1.0 + value * (1.0 - sig))

def dilated_conv(field, weight, dilation):
    chans = weight.shape[0]
    kernel = weight.astype(jnp.float32).reshape(chans, 3, 3, 3, chans).transpose(4, 0, 1, 2, 3)
    return lax.conv_general_dilated(field.astype(jnp.float32), kernel, (1, 1, 1), [(dilation, dilation)] * 3, rhs_dilation=(dilation, dilation, dilation), dimension_numbers=('NCDHW', 'OIDHW', 'NCDHW'), precision=HIGH)

def flipped(weight):
    return weight[:, ::-1, :].transpose(2, 1, 0)

def weight_grad(field, deltas, dilation):
    chans, inline_cells, depth_cells, cross_cells = field.shape
    padded = jnp.pad(field.astype(jnp.float32), ((0, 0), (dilation, dilation), (dilation, dilation), (dilation, dilation)))
    deltas32 = deltas.astype(jnp.float32)

    def one_tap(index):
        along_x = index // 9
        along_z = index // 3 % 3
        along_y = index % 3
        tap = lax.dynamic_slice(padded, (jnp.int32(0), along_x * dilation, along_z * dilation, along_y * dilation), (chans, inline_cells, depth_cells, cross_cells))
        return jnp.einsum('ixzy,toxzy->tio', tap, deltas32, precision=HIGH)
    per_tap = lax.map(one_tap, jnp.arange(27, dtype=jnp.int32))
    return per_tap.transpose(1, 2, 0, 3)

def head_cotangent(second_out, head, labels, scale):
    field = second_out.astype(jnp.float32)
    head32 = head.astype(jnp.float32)
    raw = jnp.einsum('cxzy,cn->nxzy', field, head32, precision=HIGH)
    expo = jnp.exp(capped(raw))
    prob = expo / lax.optimization_barrier(jnp.sum(expo, axis=0, keepdims=True))
    classes = jnp.arange(head.shape[1], dtype=jnp.int32)
    onehot = (labels[None] == classes[:, None, None, None]).astype(jnp.float32)
    dlog = (prob - onehot) * cap_slope(raw) * scale
    return jnp.einsum('cn,nxzy->cxzy', head32, dlog, precision=HIGH)

def trace_backward(field32, raw, expo, num, total, query, head, labels, scale):
    head32 = head.astype(jnp.float32)
    pooled = num / total[None]
    salt_raw = jnp.einsum('cxy,cn->nxy', pooled, head32, precision=HIGH)
    salt_exp = jnp.exp(capped(salt_raw))
    prob = salt_exp / lax.optimization_barrier(jnp.sum(salt_exp, axis=0, keepdims=True))
    classes = jnp.arange(head.shape[1], dtype=jnp.int32)
    onehot = (labels[None] == classes[:, None, None]).astype(jnp.float32)
    dlog = (prob - onehot) * cap_slope(salt_raw) * scale
    dvec = jnp.einsum('cn,nxy->cxy', head32, dlog, precision=HIGH)
    attn = expo / total[:, None, :]
    along = jnp.einsum('cxy,cxzy->xzy', dvec, field32, precision=HIGH)
    inner = lax.optimization_barrier(jnp.sum(dvec * pooled, axis=0))
    dscore = attn * (along - inner[:, None, :]) * cap_slope(raw)
    return attn[None] * dvec[:, :, None, :] + dscore[None] * query.astype(jnp.float32)[:, None, None, None]

def reference(features, conv1_weight, conv2_weight, fault_head, horizon_head, salt_query, salt_head, fault_labels, horizon_labels, salt_labels):
    chans, inline_cells, depth_cells, cross_cells = features.shape
    scale = 1.0 / math.sqrt(inline_cells * depth_cells * cross_cells)
    first_pre = dilated_conv(features[None], conv1_weight, D1)[0]
    first_out = (features.astype(jnp.float32) + jax.nn.silu(first_pre)).astype(jnp.bfloat16)
    second_pre = dilated_conv(first_out[None], conv2_weight, D2)[0]
    second_out = (first_out.astype(jnp.float32) + jax.nn.silu(second_pre)).astype(jnp.bfloat16)
    fault_cot = head_cotangent(second_out, fault_head, fault_labels, scale)
    horizon_cot = head_cotangent(second_out, horizon_head, horizon_labels, scale)
    field32 = second_out.astype(jnp.float32)
    raw = jnp.einsum('cxzy,c->xzy', field32, salt_query.astype(jnp.float32), precision=HIGH)
    expo = jnp.exp(capped(raw))
    total = lax.optimization_barrier(jnp.sum(expo, axis=1))
    num = jnp.einsum('xzy,cxzy->cxy', expo, field32, precision=HIGH)
    salt_cot = trace_backward(field32, raw, expo, num, total, salt_query, salt_head, salt_labels, depth_cells * scale)
    cot = jnp.stack([fault_cot, horizon_cot, salt_cot])
    second_delta = (cot * silu_slope(second_pre)[None]).astype(jnp.bfloat16)
    second_grad = weight_grad(first_out, second_delta, D2)
    first_cot = cot + dilated_conv(second_delta, flipped(conv2_weight), D2)
    first_delta = (first_cot * silu_slope(first_pre)[None]).astype(jnp.bfloat16)
    first_grad = weight_grad(features, first_delta, D1)
    grads = jnp.stack([first_grad.reshape(3, -1), second_grad.reshape(3, -1)])
    gram = jnp.einsum('bti,bui->btu', grads, grads, precision=HIGH) / (27 * C * C)
    return (grads, gram)
```

```python
import functools
import math

import jax
import jax.numpy as jnp
import numpy as np
from jax import lax
from jax.experimental import pallas as pl
from jax.experimental.pallas import tpu as pltpu
from jax.sharding import Mesh
from jax.sharding import PartitionSpec as P

MESH = pl.DeviceIdType.MESH
TILE = ("tile_0", "tile_1", "tile_2")
INLINE = ("inline_0", "inline_1")
INLINE_TILE = INLINE + TILE
D1 = 1
D2 = 2
C = 96
V = 512
CAPPING = 8.0
F32 = jnp.float32
BF16 = jnp.bfloat16
LANES = 896
HALF = 512
NORM = 27 * C * C


def row_order():
    out = np.zeros((2, HALF, 9 * C), np.float32)
    for core in range(2):
        for half in range(2):
            for first in range(4):
                for second in range(4):
                    x, y = (first, second) if half == 0 else (second, first)
                    for z in range(8):
                        for r in range(2):
                            rho = (((y % 2) * 4 + x) * 2 + half) * 2 + r
                            if rho >= 27:
                                continue
                            s, ab = divmod(rho, 9)
                            i = 12 * ((z // 2) * 2 + core) + 3 * ((z % 2) * 2 + y // 2) + s
                            row = (((half * 4 + first) * 4 + second) * 8 + z) * 2 + r
                            out[core, row, ab * C + i] = 1.0
    return out


def shifted(x, k):
    lane = lax.broadcasted_iota(jnp.int32, (x.shape[0], 128), 1) + k
    keep = (lane >= 0) & (lane < 128)
    parts = []
    for j in range(x.shape[1] // 128):
        part = pltpu.roll(x[:, j * 128 : (j + 1) * 128], (-k) % 128, 1)
        parts.append(jnp.where(keep, part, 0.0))
    return jnp.concatenate(parts, axis=1)


def dot(a, b):
    return lax.dot_general(a, b, (((1,), (0,)), ((), ())), preferred_element_type=F32)


def dot_t(a, b):
    return lax.dot_general(a, b, (((1,), (1,)), ((), ())), preferred_element_type=F32)


def capped(value):
    return CAPPING * jnp.tanh(value / CAPPING)


def cap_slope(value):
    squash = jnp.tanh(value / CAPPING)
    return 1.0 - squash * squash


def head_logits(raw, labels, scale):
    expo = [jnp.exp(capped(r)) for r in raw]
    total = functools.reduce(lambda a, b: a + b, expo)
    return [
        (e / total - (labels == n).astype(F32)) * cap_slope(r) * scale
        for n, (e, r) in enumerate(zip(expo, raw))
    ]


def three_parts(g):
    hi = g.astype(BF16)
    rest = g - hi.astype(F32)
    mid = rest.astype(BF16)
    low = (rest - mid.astype(F32)).astype(BF16)
    return jnp.concatenate([hi, mid, low], axis=0)


def kernel(
    scale,
    depth_scale,
    feat_ref,
    w1_ref,
    w2_ref,
    w2t_ref,
    heads_ref,
    spread_ref,
    order_ref,
    fault_ref,
    horizon_ref,
    salt_ref,
    out_ref,
    gram_ref,
    fpad,
    f91,
    f92,
    slope9,
    g9,
    d9,
    slope1,
    cotc,
    amat,
    fsend,
    draw,
    dpart,
    dsh,
    pbuf,
    o32,
    s1src,
    s1recv,
    s2src,
    s2recv,
    r16,
    s3src,
    s3recv,
    tbuf,
    pool_x,
    pool_mine,
    pool_z,
    gram_x,
    gram_z,
    ssem,
    rsem,
):
    zh, core, zl, y, x = [lax.axis_index(a) for a in INLINE_TILE]
    inline = zh * 2 + core
    tile = zl * 16 + y * 4 + x
    z = zh * 2 + zl
    xy = y * 4 + x
    zc = z * 2 + core
    yhi, ylo = y // 2, y % 2
    p = ylo * 4 + x

    sem_count = [0]
    sent = []

    def send(src, dst, device):
        n = sem_count[0]
        sem_count[0] += 1
        copy = pltpu.make_async_remote_copy(
            src_ref=src,
            dst_ref=dst,
            send_sem=ssem.at[n],
            recv_sem=rsem.at[n],
            device_id=device,
            device_id_type=MESH,
        )
        copy.start()
        sent.append(copy)
        return copy

    def at_grid(dx, dz):
        i = (inline + dx + 8) % 8
        t = (tile + dz + 32) % 32
        return (i // 2, i % 2, t // 16, (t // 4) % 4, t % 4)

    around = [(dx, dz) for dx in (-1, 0, 1) for dz in (-1, 0, 1) if (dx, dz) != (0, 0)]
    halo_to = {d: at_grid(*d) for d in around}

    def plane(k):
        q = (xy + k) % 16
        return (zh, core, zl, q // 4, q % 4)

    def column(k):
        q = (zc + k) % 16
        return (q // 4, q % 2, (q // 2) % 2, y, x)

    partner = (zh, 1 - core, zl, y, x)

    for li in range(2):
        s3src[li] = jnp.zeros(s3src.shape[1:], F32)
    dsh[864:896, :] = jnp.zeros((32, 1024), BF16)

    for cell in range(4):
        fpad[(cell // 2 + 1) * 4 + cell % 2 + 1] = feat_ref[cell]

    barrier = pltpu.get_barrier_semaphore()
    greeted = [halo_to[d] for d in around] + [plane(k) for k in range(1, 16)]
    greeted += [column(k) for k in range(1, 16)]
    for device in greeted:
        pl.semaphore_signal(barrier, inc=1, device_id=device, device_id_type=MESH)
    pl.semaphore_wait(barrier, len(greeted))

    copies = []
    for dx, dz in around:
        for cx in (0, 1) if dx == 0 else ((1,) if dx == 1 else (0,)):
            for cz in (0, 1) if dz == 0 else ((1,) if dz == 1 else (0,)):
                src = (cx + 1) * 4 + cz + 1
                dst = (cx - 2 * dx + 1) * 4 + (cz - 2 * dz + 1)
                copies.append(send(fpad.at[src], fpad.at[dst], halo_to[dx, dz]))
    for copy in copies:
        copy.wait_recv()

    low_x, high_x = inline == 0, inline == 7
    low_z, high_z = tile == 0, tile == 31
    none = jnp.zeros((C, 128), BF16)

    @pl.when(low_x)
    def _():
        for j in range(4):
            fpad[j] = none

    @pl.when(high_x)
    def _():
        for j in range(4):
            fpad[12 + j] = none

    @pl.when(low_z)
    def _():
        for j in range(4):
            fpad[4 * j] = none

    @pl.when(high_z)
    def _():
        for j in range(4):
            fpad[4 * j + 3] = none

    for a in range(3):
        for b in range(3):
            for cell in range(4):
                row = (a * 3 + b) * C
                f91[row : row + C, cell * 128 : (cell + 1) * 128] = fpad[
                    (cell // 2 + a) * 4 + cell % 2 + b
                ]

    def taps_added(pbuf, d):
        return pbuf[C : 2 * C, :] + shifted(pbuf[0:C, :], -d) + shifted(pbuf[2 * C :, :], d)

    pbuf[...] = dot(w1_ref[...], f91[...])
    pre = taps_added(pbuf, D1)
    sig = jax.nn.sigmoid(pre)
    own = jnp.concatenate([feat_ref[cell] for cell in range(4)], axis=1).astype(F32)
    f92[4] = (own + pre * sig).astype(BF16)
    slope1[...] = sig * (1.0 + pre * (1.0 - sig))

    def blocks_around(buffer):
        made = []
        for dx, dz in around:
            slot = (1 - dx) * 3 + (1 - dz)
            made.append(send(buffer.at[4], buffer.at[slot], halo_to[dx, dz]))
        return made

    def clear_outside(buffer):
        zeros = jnp.zeros(buffer.shape[1:], buffer.dtype)

        @pl.when(low_x)
        def _():
            for j in range(3):
                buffer[j] = zeros

        @pl.when(high_x)
        def _():
            for j in range(3):
                buffer[6 + j] = zeros

        @pl.when(low_z)
        def _():
            for j in range(3):
                buffer[3 * j] = zeros

        @pl.when(high_z)
        def _():
            for j in range(3):
                buffer[3 * j + 2] = zeros

    def rows_exchanged(li, field):
        amat[li, :, 0:V] = dot(order_ref[core], field).astype(BF16)
        fsend[li] = dot(order_ref[1 - core], field).astype(BF16)
        return send(fsend.at[li], amat.at[li, :, V : 2 * V], partner)

    copies = blocks_around(f92)
    row_copy = [rows_exchanged(0, f91[...])]
    for copy in copies:
        copy.wait_recv()
    clear_outside(f92)

    field9 = f92[...].reshape(9 * C, V)
    pbuf[...] = dot(w2_ref[...], field9)
    pre = taps_added(pbuf, D2)
    sig = jax.nn.sigmoid(pre)
    second = (f92[4].astype(F32) + pre * sig).astype(BF16)
    slope2 = sig * (1.0 + pre * (1.0 - sig))
    slope9[4] = slope2.astype(BF16)
    slope_copies = blocks_around(slope9)

    raw = dot(heads_ref[...], second)
    rows = [raw[n : n + 1, :] for n in range(9)]
    expo = jnp.exp(capped(rows[6]))

    def depth_sum(r):
        return jnp.concatenate(
            [r[:, 0:128] + r[:, 128:256], r[:, 256:384] + r[:, 384:512]], axis=1
        )

    zero_row = jnp.zeros((1, 256), F32)
    partial = [depth_sum(expo), depth_sum(expo * rows[7]), depth_sum(expo * rows[8])]
    pool_x[xy] = jnp.concatenate(partial + [zero_row] * 5, axis=0)
    copies = [send(pool_x.at[xy], pool_x.at[xy], plane(k)) for k in range(1, 16)]
    logits = head_logits(rows[0:2], fault_ref[...], scale)
    logits += head_logits(rows[2:6], horizon_ref[...], scale)
    row_copy.append(rows_exchanged(1, field9))
    for copy in copies:
        copy.wait_recv()
    pooled = pool_x[0]
    for j in range(1, 16):
        pooled = pooled + pool_x[j]
    pool_mine[...] = pooled
    copy = send(pool_mine, pool_z, (zh, core, 1 - zl, y, x))
    copy.wait_recv()
    pooled = pool_mine[...] + pool_z[...]
    total = pooled[0:1, :]
    salt_raw = [pooled[1:2, :] / total, pooled[2:3, :] / total]
    salt_log = head_logits(salt_raw, salt_ref[...], depth_scale)
    inner = salt_log[0] * salt_raw[0] + salt_log[1] * salt_raw[1]

    def per_cell(r):
        return jnp.concatenate([r[:, 0:128], r[:, 0:128], r[:, 128:256], r[:, 128:256]], axis=1)

    attn = expo / per_cell(total)
    wide = [per_cell(r) for r in salt_log]
    along = wide[0] * rows[7] + wide[1] * rows[8]
    dscore = attn * (along - per_cell(inner)) * cap_slope(rows[6])
    voxel = logits + [dscore, attn * wide[0], attn * wide[1]]
    g = jnp.concatenate(voxel + [jnp.zeros((7, V), F32)], axis=0)
    g9[4] = g
    g_copies = blocks_around(g9)

    cot = dot(spread_ref[...], three_parts(g))
    cotc[...] = cot
    for t in range(3):
        delta = (cot[t * C : (t + 1) * C, :] * slope2).astype(BF16)
        d9[t, 4 * C : 5 * C, :] = delta
        draw[1, t * C : (t + 1) * C, :] = delta

    def shifted_deltas(ref, at, d):
        for t in range(3):
            mid = ref[t * C : (t + 1) * C, :]
            wide = mid.astype(F32)
            low = shifted(wide, d).astype(BF16)
            high = shifted(wide, -d).astype(BF16)
            cols = slice(at, at + V)
            dsh[t * 256 : t * 256 + 96, cols] = low
            dsh[t * 256 + 96 : t * 256 + 192, cols] = mid
            dsh[t * 256 + 192 : t * 256 + 256, cols] = high[0:64, :]
            dsh[768 + 32 * t : 800 + 32 * t, cols] = high[64:96, :]

    def at_x(k):
        return (zh, core, zl, y, (x + k) % 4)

    def at_y(k):
        return (zh, core, zl, (y + k) % 4, x)

    first_at, first_of = (at_x, at_y), (x, y)
    second_at, second_of = (at_y, at_x), (y, x)

    def stage1(li, d, delta_copy):
        shifted_deltas(draw.at[li], 0, d)
        delta_copy.wait_recv()
        shifted_deltas(dpart.at[li], V, d)
        row_copy[li].wait_recv()
        made = []
        for h in range(2):
            part = slice(h * 256, (h + 1) * 256)
            prod = dot_t(amat[li, part, :], dsh[...])
            o32[li, part, :] = prod
            s1src[li, part, :] = prod.astype(BF16)
            for k in range(1, 4):
                to = h * 256 + ((first_of[h] + k) % 4) * 64
                src = s1src.at[li, pl.ds(pl.multiple_of(to, 64), 64), :]
                made.append(send(src, s1recv.at[li, h, k - 1], first_at[h](k)))
        return made

    def stage2(li, copies):
        for copy in copies:
            copy.wait_recv()
        made = []
        for h in range(2):
            mine = pl.multiple_of(h * 256 + first_of[h] * 64, 64)
            part = o32[li, pl.ds(mine, 64), :]
            for k in range(3):
                part = part + s1recv[li, h, k].astype(F32)
            s2src[li, h] = part
            for k in range(1, 4):
                to = pl.multiple_of(((second_of[h] + k) % 4) * 16, 16)
                src = s2src.at[li, h, pl.ds(to, 16), :]
                made.append(send(src, s2recv.at[li, h, k - 1], second_at[h](k)))
        return made

    def stage3(li, copies):
        for copy in copies:
            copy.wait_recv()
        for h in range(2):
            mine = pl.multiple_of(second_of[h] * 16, 16)
            part = s2src[li, h, pl.ds(mine, 16), :]
            for k in range(3):
                part = part + s2recv[li, h, k]
            r16[...] = part
            for zz in range(8):
                for r in range(2):
                    row = zz * 2 + r
                    for lane in range(7):
                        s3src[li, zz, h * 2 + r, lane : lane + 1, :] = r16[
                            row : row + 1, lane * 128 : (lane + 1) * 128
                        ]
        made = []
        for k in range(1, 8):
            q = (z + k) % 8
            made.append(send(s3src.at[li, q], s3recv.at[li, k - 1], (q // 2, core, q % 2, y, x)))
        return made

    def stage4(li, copies):
        for copy in copies:
            copy.wait_recv()
        part = s3src[li, z]
        for k in range(7):
            part = part + s3recv[li, k]
        tbuf[li, p] = part
        made = []
        for k in range(1, 8):
            q = (p + k) % 8
            device = (zh, core, zl, yhi * 2 + q // 4, q % 4)
            made.append(send(tbuf.at[li, p], tbuf.at[li, p], device))
        return part, made

    def gram_rows(part):
        lane = lax.broadcasted_iota(jnp.int32, (4, 128), 1)
        tail = part[:, 6, :]
        values = []
        for t in range(3):
            rest = tail if t == 0 else pltpu.roll(tail, 128 - 32 * t, 1)
            rest = jnp.where(lane < 32, rest, 0.0)
            values.append((part[:, 2 * t, :], part[:, 2 * t + 1, :], rest))
        found = []
        for t in range(3):
            for u in range(t, 3):
                prod = sum(a * b for a, b in zip(values[t], values[u]))
                found.append(jnp.sum(prod, axis=0, keepdims=True))
        return found

    copy = send(draw.at[1], dpart.at[1], partner)
    reduce2 = stage1(1, D2, copy)

    for copy in slope_copies:
        copy.wait_recv()
    clear_outside(slope9)
    for copy in g_copies:
        copy.wait_recv()
    for s in range(9):
        if s == 4:
            continue
        cot = dot(spread_ref[...], three_parts(g9[s]))
        slope = slope9[s].astype(F32)
        for t in range(3):
            d9[t, (8 - s) * C : (9 - s) * C, :] = (cot[t * C : (t + 1) * C, :] * slope).astype(
                BF16
            )
    for t in range(3):
        pbuf[...] = dot(w2t_ref[...], d9[t])
        cot = cotc[t * C : (t + 1) * C, :] + taps_added(pbuf, -D2)
        draw[0, t * C : (t + 1) * C, :] = (cot * slope1[...]).astype(BF16)
    copy = send(draw.at[0], dpart.at[0], partner)
    reduce2 = stage2(1, reduce2)
    reduce1 = stage1(0, D1, copy)
    reduce2 = stage3(1, reduce2)
    reduce1 = stage2(0, reduce1)
    part2, spread2 = stage4(1, reduce2)
    found2 = gram_rows(part2)
    reduce1 = stage3(0, reduce1)
    part1, spread1 = stage4(0, reduce1)
    found = gram_rows(part1) + found2 + [jnp.zeros((4, 128), F32)]
    gram_x[xy] = jnp.concatenate(found, axis=0)
    copies = [send(gram_x.at[xy], gram_x.at[xy], plane(k)) for k in range(1, 16)]
    for copy in copies:
        copy.wait_recv()
    part = gram_x[0]
    for j in range(1, 16):
        part = part + gram_x[j]
    gram_z[zc] = part
    copies = [send(gram_z.at[zc], gram_z.at[zc], column(k)) for k in range(1, 16)]
    for copy in spread2 + spread1:
        copy.wait_recv()
    out_ref[...] = tbuf[...]
    for copy in copies:
        copy.wait_recv()
    part = gram_z[0]
    for j in range(1, 16):
        part = part + gram_z[j]
    gram_ref[...] = part
    for copy in sent:
        copy.wait_send()


def on_device(
    features,
    conv1_weight,
    conv2_weight,
    fault_head,
    horizon_head,
    salt_query,
    salt_head,
    fault_labels,
    horizon_labels,
    salt_labels,
):
    chans, inline_cells, depth_cells, cross_cells = features.shape
    depth_total = depth_cells * lax.axis_size(TILE)
    scale = 1.0 / math.sqrt(inline_cells * lax.axis_size(INLINE) * depth_total * cross_cells)
    cells = features.transpose(1, 2, 0, 3).reshape(4, C, 128)
    w1 = conv1_weight.reshape(C, 9, 3, C).transpose(2, 3, 1, 0).reshape(3 * C, 9 * C)
    w2 = conv2_weight.reshape(C, 9, 3, C).transpose(2, 3, 1, 0).reshape(3 * C, 9 * C)
    w2t = conv2_weight.reshape(C, 9, 3, C).transpose(2, 0, 1, 3).reshape(3 * C, 9 * C)
    heads = jnp.concatenate(
        [fault_head, horizon_head, salt_query[:, None], salt_head, jnp.zeros((C, 7), BF16)], axis=1
    )
    task = np.zeros((3, 16), np.float32)
    task[0, 0:2] = 1.0
    task[1, 2:6] = 1.0
    task[2, 6:9] = 1.0
    spread = (heads[None] * jnp.asarray(task, BF16)[:, None, :]).reshape(3 * C, 16)
    spread = jnp.concatenate([spread] * 3, axis=1)
    order = jnp.asarray(row_order(), BF16)

    scratch = [
        pltpu.VMEM((16, C, 128), BF16),
        pltpu.VMEM((9 * C, V), BF16),
        pltpu.VMEM((9, C, V), BF16),
        pltpu.VMEM((9, C, V), BF16),
        pltpu.VMEM((9, 16, V), F32),
        pltpu.VMEM((3, 9 * C, V), BF16),
        pltpu.VMEM((C, V), F32),
        pltpu.VMEM((3 * C, V), F32),
        pltpu.VMEM((2, HALF, 2 * V), BF16),
        pltpu.VMEM((2, HALF, V), BF16),
        pltpu.VMEM((2, 3 * C, V), BF16),
        pltpu.VMEM((2, 3 * C, V), BF16),
        pltpu.VMEM((LANES, 2 * V), BF16),
        pltpu.VMEM((3 * C, V), F32),
        pltpu.VMEM((2, HALF, LANES), F32),
        pltpu.VMEM((2, HALF, LANES), BF16),
        pltpu.VMEM((2, 2, 3, 64, LANES), BF16),
        pltpu.VMEM((2, 2, 64, LANES), F32),
        pltpu.VMEM((2, 2, 3, 16, LANES), F32),
        pltpu.VMEM((16, LANES), F32),
        pltpu.VMEM((2, 8, 4, 8, 128), F32),
        pltpu.VMEM((2, 7, 4, 8, 128), F32),
        pltpu.VMEM((2, 8, 4, 8, 128), F32),
        pltpu.VMEM((16, 8, 256), F32),
        pltpu.VMEM((8, 256), F32),
        pltpu.VMEM((8, 256), F32),
        pltpu.VMEM((16, 16, 128), F32),
        pltpu.VMEM((16, 16, 128), F32),
        pltpu.SemaphoreType.DMA((160,)),
        pltpu.SemaphoreType.DMA((160,)),
    ]
    whole = pl.BlockSpec(memory_space=pltpu.VMEM)
    units, gram_rows = pl.pallas_call(
        functools.partial(kernel, scale, depth_total * scale),
        out_shape=(
            jax.ShapeDtypeStruct((2, 8, 4, 8, 128), F32),
            jax.ShapeDtypeStruct((16, 128), F32),
        ),
        in_specs=[whole] * 10,
        out_specs=(whole, whole),
        scratch_shapes=scratch,
        compiler_params=pltpu.CompilerParams(
            collective_id=0, has_side_effects=True, vmem_limit_bytes=48 * 1024 * 1024
        ),
    )(
        cells,
        w1,
        w2,
        w2t,
        heads.T,
        spread,
        order,
        fault_labels.reshape(1, V),
        horizon_labels.reshape(1, V),
        salt_labels.reshape(1, 256),
    )
    p = (lax.axis_index("tile_1") % 2) * 4 + lax.axis_index("tile_2")
    start = (27 * p) // 8
    mine = lax.dynamic_slice_in_dim(units.reshape(2, 32, 1024), start, 5, 1)
    main = mine[:, :, 0:768].reshape(2, 5, 3, 256)
    tail = mine[:, :, 768:864].reshape(2, 5, 3, 32)
    entries = jnp.concatenate([main, tail], axis=3).transpose(0, 2, 1, 3).reshape(2, 3, 5 * 288)
    grads = lax.dynamic_slice_in_dim(entries, 36 * ((27 * p) % 8), NORM // 256, 2)
    sums = jnp.sum(gram_rows[0:12, :], axis=1).reshape(2, 6) / NORM
    gram = sums[:, np.array([0, 1, 2, 1, 3, 4, 2, 4, 5])].reshape(2, 3, 3)
    return (grads, gram)


def solution(mesh):
    split = Mesh(
        mesh.devices.reshape(4, 2, 2, 4, 4), ("inline_0", "inline_1", "tile_0", "tile_1", "tile_2")
    )
    return jax.shard_map(
        on_device,
        mesh=split,
        in_specs=(
            P(None, INLINE, TILE, None),
            P(),
            P(),
            P(),
            P(),
            P(),
            P(),
            P(INLINE, TILE, None),
            P(INLINE, TILE, None),
            P(INLINE, None),
        ),
        out_specs=(P(None, None, INLINE_TILE), P()),
        check_vma=False,
    )
```

```python
import functools
import math

import jax
import jax.numpy as jnp
import numpy as np
from jax import lax
from jax.experimental import pallas as pl
from jax.experimental.pallas import tpu as pltpu
from jax.sharding import Mesh
from jax.sharding import PartitionSpec as P

MESH = pl.DeviceIdType.MESH
TILE = ("tile_0", "tile_1", "tile_2")
INLINE = ("inline_0", "inline_1")
INLINE_TILE = INLINE + TILE
D1 = 1
D2 = 2
C = 96
V = 512
CAPPING = 8.0
F32 = jnp.float32
BF16 = jnp.bfloat16
LANES = 896
HALF = 512
NORM = 27 * C * C


def row_order():
    out = np.zeros((2, HALF, 9 * C), np.float32)
    for core in range(2):
        for half in range(2):
            for first in range(4):
                for second in range(4):
                    x, y = (first, second) if half == 0 else (second, first)
                    for z in range(8):
                        for r in range(2):
                            rho = (((y % 2) * 4 + x) * 2 + half) * 2 + r
                            if rho >= 27:
                                continue
                            s, ab = divmod(rho, 9)
                            i = 12 * ((z // 2) * 2 + core) + 3 * ((z % 2) * 2 + y // 2) + s
                            row = (((half * 4 + first) * 4 + second) * 8 + z) * 2 + r
                            out[core, row, ab * C + i] = 1.0
    return out


def shifted(x, k):
    lane = lax.broadcasted_iota(jnp.int32, (x.shape[0], 128), 1) + k
    keep = (lane >= 0) & (lane < 128)
    parts = []
    for j in range(x.shape[1] // 128):
        part = pltpu.roll(x[:, j * 128 : (j + 1) * 128], (-k) % 128, 1)
        parts.append(jnp.where(keep, part, 0.0))
    return jnp.concatenate(parts, axis=1)


def dot(a, b):
    return lax.dot_general(a, b, (((1,), (0,)), ((), ())), preferred_element_type=F32)


def dot_t(a, b):
    return lax.dot_general(a, b, (((1,), (1,)), ((), ())), preferred_element_type=F32)


def capped(value):
    return CAPPING * jnp.tanh(value / CAPPING)


def cap_slope(value):
    squash = jnp.tanh(value / CAPPING)
    return 1.0 - squash * squash


def head_logits(raw, labels, scale):
    expo = [jnp.exp(capped(r)) for r in raw]
    total = functools.reduce(lambda a, b: a + b, expo)
    return [
        (e / total - (labels == n).astype(F32)) * cap_slope(r) * scale
        for n, (e, r) in enumerate(zip(expo, raw))
    ]


def three_parts(g):
    hi = g.astype(BF16)
    rest = g - hi.astype(F32)
    mid = rest.astype(BF16)
    low = (rest - mid.astype(F32)).astype(BF16)
    return jnp.concatenate([hi, mid, low], axis=0)


def kernel(
    scale,
    depth_scale,
    feat_ref,
    w1_hbm,
    w2_hbm,
    heads_ref,
    order_hbm,
    fault_ref,
    horizon_ref,
    salt_ref,
    out_ref,
    gram_ref,
    raw_w,
    order_ref,
    w1_ref,
    w2_ref,
    w2t_ref,
    spread_ref,
    fpad,
    f91,
    f92,
    slope9,
    g9,
    d9,
    slope1,
    cotc,
    amat,
    fsend,
    draw,
    dpart,
    dsh,
    pbuf,
    o32,
    s1src,
    s1recv,
    s2sum,
    s2src,
    s2recv,
    r16,
    s3sum,
    s3src,
    s3recv,
    tbuf,
    pool_x,
    pool_y,
    gram_x,
    gram_z,
    gram_y,
    lsem,
    ssem,
    rsem,
):
    zh, core, zl, y, x = [lax.axis_index(a) for a in INLINE_TILE]
    inline = zh * 2 + core
    tile = zl * 16 + y * 4 + x
    z = zh * 2 + zl
    yhi, ylo = y // 2, y % 2
    p = ylo * 4 + x

    sem_count = [0]
    sent = []

    def send(src, dst, device):
        n = sem_count[0]
        sem_count[0] += 1
        copy = pltpu.make_async_remote_copy(
            src_ref=src,
            dst_ref=dst,
            send_sem=ssem.at[n],
            recv_sem=rsem.at[n],
            device_id=device,
            device_id_type=MESH,
        )
        copy.start()
        sent.append(copy)
        return copy

    def at_grid(dx, dz):
        i = (inline + dx + 8) % 8
        t = (tile + dz + 32) % 32
        return (i // 2, i % 2, t // 16, (t // 4) % 4, t % 4)

    around = [(dx, dz) for dx in (-1, 0, 1) for dz in (-1, 0, 1) if (dx, dz) != (0, 0)]
    halo_to = {d: at_grid(*d) for d in around}

    partner = (zh, 1 - core, zl, y, x)

    def at_x(k):
        return (zh, core, zl, y, (x + k) % 4)

    def at_y(k):
        return (zh, core, zl, (y + k) % 4, x)

    def at_z(k):
        q = (z + k) % 8
        return (q // 2, core, q % 2, y, x)

    def at_eight(k):
        q = (p + k) % 8
        return (zh, core, zl, yhi * 2 + q // 4, q % 4)

    def at_depth(k):
        q = (zl * 2 + yhi + k) % 4
        return (zh, core, q // 2, (q % 2) * 2 + ylo, x)

    def at_unit(k):
        q = (core * 2 + yhi + k) % 4
        return (zh, q // 2, zl, (q % 2) * 2 + ylo, x)

    loads = [
        pltpu.make_async_copy(src, dst, lsem.at[n])
        for n, (src, dst) in enumerate(
            ((w1_hbm, raw_w.at[0]), (w2_hbm, raw_w.at[1]), (order_hbm, order_ref))
        )
    ]
    for load in loads:
        load.start()

    barrier = pltpu.get_barrier_semaphore()
    greeted = [halo_to[d] for d in around]
    greeted += [at_eight(k) for k in range(1, 8)] + [at_z(k) for k in range(1, 8)]
    greeted += [at_y(k) for k in range(1, 4)]
    greeted += [at_depth(k) for k in range(1, 4)] + [at_unit(k) for k in range(1, 4)]
    for device in greeted:
        pl.semaphore_signal(barrier, inc=1, device_id=device, device_id_type=MESH)

    for cell in range(4):
        fpad[(cell // 2 + 1) * 4 + cell % 2 + 1] = feat_ref[cell]
    for li in range(2):
        s3sum[li] = jnp.zeros(s3sum.shape[1:], F32)
    dsh[864:896, :] = jnp.zeros((32, 1024), BF16)

    eye = (
        lax.broadcasted_iota(jnp.int32, (C, C), 0) == lax.broadcasted_iota(jnp.int32, (C, C), 1)
    ).astype(BF16)

    def transposed_weight(n, out):
        for c in range(3):
            rows = jnp.concatenate([raw_w[n, ab * 3 + c] for ab in range(9)], axis=0)
            out[c * C : (c + 1) * C, :] = dot_t(eye, rows).astype(BF16)

    pl.semaphore_wait(barrier, len(greeted))

    copies = []
    for dx, dz in around:
        for cx in (0, 1) if dx == 0 else ((1,) if dx == 1 else (0,)):
            for cz in (0, 1) if dz == 0 else ((1,) if dz == 1 else (0,)):
                src = (cx + 1) * 4 + cz + 1
                dst = (cx - 2 * dx + 1) * 4 + (cz - 2 * dz + 1)
                copies.append(send(fpad.at[src], fpad.at[dst], halo_to[dx, dz]))
    loads[0].wait()
    transposed_weight(0, w1_ref)
    for copy in copies:
        copy.wait_recv()

    low_x, high_x = inline == 0, inline == 7
    low_z, high_z = tile == 0, tile == 31
    none = jnp.zeros((C, 128), BF16)

    @pl.when(low_x)
    def _():
        for j in range(4):
            fpad[j] = none

    @pl.when(high_x)
    def _():
        for j in range(4):
            fpad[12 + j] = none

    @pl.when(low_z)
    def _():
        for j in range(4):
            fpad[4 * j] = none

    @pl.when(high_z)
    def _():
        for j in range(4):
            fpad[4 * j + 3] = none

    for a in range(3):
        for b in range(3):
            for cell in range(4):
                row = (a * 3 + b) * C
                f91[row : row + C, cell * 128 : (cell + 1) * 128] = fpad[
                    (cell // 2 + a) * 4 + cell % 2 + b
                ]

    def taps_added(pbuf, d):
        return pbuf[C : 2 * C, :] + shifted(pbuf[0:C, :], -d) + shifted(pbuf[2 * C :, :], d)

    pbuf[...] = dot(w1_ref[...], f91[...])
    pre = taps_added(pbuf, D1)
    sig = jax.nn.sigmoid(pre)
    own = jnp.concatenate([feat_ref[cell] for cell in range(4)], axis=1).astype(F32)
    f92[4] = (own + pre * sig).astype(BF16)
    slope1[...] = sig * (1.0 + pre * (1.0 - sig))

    def blocks_around(buffer):
        made = []
        for dx, dz in around:
            slot = (1 - dx) * 3 + (1 - dz)
            made.append(send(buffer.at[4], buffer.at[slot], halo_to[dx, dz]))
        return made

    zs = 2 * core - 1
    zrow = (zs + 1) * 3

    def blocks_sent(buffer):
        own = buffer.at[4]
        far = send(own, buffer.at[(1 - zs) * 3 + 1], at_grid(zs, 0))
        up = send(own, buffer.at[3], halo_to[0, 1])
        down = send(own, buffer.at[5], halo_to[0, -1])
        near = send(own, buffer.at[zrow + 1], partner)
        return far, up, down, near

    def blocks_passed_on(buffer, first):
        far, up, down, near = first
        far.wait_recv()
        passed = [
            send(buffer.at[zrow + 1], buffer.at[zrow], halo_to[0, 1]),
            send(buffer.at[zrow + 1], buffer.at[zrow + 2], halo_to[0, -1]),
        ]
        up.wait_recv()
        passed.append(send(buffer.at[3], buffer.at[zrow], partner))
        down.wait_recv()
        passed.append(send(buffer.at[5], buffer.at[zrow + 2], partner))
        return near, passed

    def blocks_arrived(buffer, second):
        near, passed = second
        near.wait_recv()
        for copy in passed:
            copy.wait_recv()
        for copy in passed:
            copy.wait_send()
        sent[:] = [copy for copy in sent if not any(copy is done for done in passed)]
        clear_outside(buffer)

    def clear_outside(buffer):
        zeros = jnp.zeros(buffer.shape[1:], buffer.dtype)

        @pl.when(low_x)
        def _():
            for j in range(3):
                buffer[j] = zeros

        @pl.when(high_x)
        def _():
            for j in range(3):
                buffer[6 + j] = zeros

        @pl.when(low_z)
        def _():
            for j in range(3):
                buffer[3 * j] = zeros

        @pl.when(high_z)
        def _():
            for j in range(3):
                buffer[3 * j + 2] = zeros

    def rows_exchanged(li, field):
        amat[li, :, 0:V] = dot(order_ref[core], field).astype(BF16)
        fsend[li] = dot(order_ref[1 - core], field).astype(BF16)
        return send(fsend.at[li], amat.at[li, :, V : 2 * V], partner)

    blocks = blocks_sent(f92)
    loads[2].wait()
    row_copy = [rows_exchanged(0, f91[...])]
    blocks = blocks_passed_on(f92, blocks)
    loads[1].wait()
    transposed_weight(1, w2_ref)
    for c in range(3):
        for ab in range(9):
            w2t_ref[c * C : (c + 1) * C, ab * C : (ab + 1) * C] = raw_w[1, ab * 3 + c]
    heads = heads_ref[...]
    lane = lax.broadcasted_iota(jnp.int32, (C, 16), 1)
    of_task = ((lane >= 0) & (lane < 2), (lane >= 2) & (lane < 6), (lane >= 6) & (lane < 9))
    spread = [jnp.where(of, heads.astype(F32), 0.0) for of in of_task]
    spread = jnp.concatenate(spread, axis=0).astype(BF16)
    again = lax.broadcasted_iota(jnp.int32, (16, 48), 1) % 16
    again = (again == lax.broadcasted_iota(jnp.int32, (16, 48), 0)).astype(BF16)
    spread_ref[...] = dot(spread, again).astype(BF16)
    blocks_arrived(f92, blocks)

    field9 = f92[...].reshape(9 * C, V)
    pbuf[...] = dot(w2_ref[...], field9)
    pre = taps_added(pbuf, D2)
    sig = jax.nn.sigmoid(pre)
    second = (f92[4].astype(F32) + pre * sig).astype(BF16)
    slope2 = sig * (1.0 + pre * (1.0 - sig))
    slope9[4] = slope2.astype(BF16)

    raw = lax.dot_general(heads, second, (((0,), (0,)), ((), ())), preferred_element_type=F32)
    rows = [raw[n : n + 1, :] for n in range(9)]
    expo = jnp.exp(capped(rows[6]))

    def depth_sum(r):
        return jnp.concatenate(
            [r[:, 0:128] + r[:, 128:256], r[:, 256:384] + r[:, 384:512]], axis=1
        )

    zero_row = jnp.zeros((1, 256), F32)
    partial = [depth_sum(expo), depth_sum(expo * rows[7]), depth_sum(expo * rows[8])]
    pool_x[p] = jnp.concatenate(partial + [zero_row] * 5, axis=0)
    copies = [send(pool_x.at[p], pool_x.at[p], at_eight(k)) for k in range(1, 8)]
    blocks = blocks_sent(slope9)
    fault = jnp.concatenate([fault_ref[a, b : b + 1, :] for a in (0, 1) for b in (0, 1)], axis=1)
    horizon = jnp.concatenate(
        [horizon_ref[a, b : b + 1, :] for a in (0, 1) for b in (0, 1)], axis=1
    )
    salt = jnp.concatenate([salt_ref[0:1, :], salt_ref[1:2, :]], axis=1)
    logits = head_logits(rows[0:2], fault, scale)
    logits += head_logits(rows[2:6], horizon, scale)
    for copy in copies:
        copy.wait_recv()
    pooled = pool_x[0]
    for j in range(1, 8):
        pooled = pooled + pool_x[j]
    quarter = zl * 2 + yhi
    pool_y[quarter] = pooled
    copies = [send(pool_y.at[quarter], pool_y.at[quarter], at_depth(k)) for k in range(1, 4)]
    blocks = blocks_passed_on(slope9, blocks)
    row_copy.append(rows_exchanged(1, field9))
    for copy in copies:
        copy.wait_recv()
    pooled = (pool_y[0] + pool_y[1]) + (pool_y[2] + pool_y[3])
    total = pooled[0:1, :]
    salt_raw = [pooled[1:2, :] / total, pooled[2:3, :] / total]
    salt_log = head_logits(salt_raw, salt, depth_scale)
    inner = salt_log[0] * salt_raw[0] + salt_log[1] * salt_raw[1]

    def per_cell(r):
        return jnp.concatenate([r[:, 0:128], r[:, 0:128], r[:, 128:256], r[:, 128:256]], axis=1)

    attn = expo / per_cell(total)
    wide = [per_cell(r) for r in salt_log]
    along = wide[0] * rows[7] + wide[1] * rows[8]
    dscore = attn * (along - per_cell(inner)) * cap_slope(rows[6])
    voxel = logits + [dscore, attn * wide[0], attn * wide[1]]
    g = jnp.concatenate(voxel + [jnp.zeros((7, V), F32)], axis=0)
    g9[4] = g
    g_copies = blocks_around(g9)

    cot = dot(spread_ref[...], three_parts(g))
    cotc[...] = cot
    for t in range(3):
        delta = (cot[t * C : (t + 1) * C, :] * slope2).astype(BF16)
        d9[t, 4 * C : 5 * C, :] = delta
        draw[1, t * C : (t + 1) * C, :] = delta

    def shifted_deltas(ref, at, d):
        for t in range(3):
            mid = ref[t * C : (t + 1) * C, :]
            wide = mid.astype(F32)
            low = shifted(wide, d).astype(BF16)
            high = shifted(wide, -d).astype(BF16)
            cols = slice(at, at + V)
            dsh[t * 256 : t * 256 + 96, cols] = low
            dsh[t * 256 + 96 : t * 256 + 192, cols] = mid
            dsh[t * 256 + 192 : t * 256 + 256, cols] = high[0:64, :]
            dsh[768 + 32 * t : 800 + 32 * t, cols] = high[64:96, :]

    first_at, first_of = (at_x, at_y), (x, y)
    second_at, second_of = (at_y, at_x), (y, x)

    def stage1(li, d, delta_copies):
        shifted_deltas(draw.at[li], 0, d)
        for copy in delta_copies:
            copy.wait_recv()
        shifted_deltas(dpart.at[li], V, d)
        row_copy[li].wait_recv()
        made = []
        for h in range(2):
            part = slice(h * 256, (h + 1) * 256)
            prod = dot_t(amat[li, part, :], dsh[...])
            o32[li, part, :] = prod
            s1src[li, part, :] = prod.astype(BF16)
            for k in range(1, 4):
                to = h * 256 + ((first_of[h] + k) % 4) * 64
                src = s1src.at[li, pl.ds(pl.multiple_of(to, 64), 64), :]
                made.append(send(src, s1recv.at[li, h, k - 1], first_at[h](k)))
        return made

    def stage2(li, copies):
        for copy in copies:
            copy.wait_recv()
        made = []
        for h in range(2):
            mine = pl.multiple_of(h * 256 + first_of[h] * 64, 64)
            part = o32[li, pl.ds(mine, 64), :]
            for k in range(3):
                part = part + s1recv[li, h, k].astype(F32)
            s2sum[li, h] = part
            s2src[li, h] = part.astype(BF16)
            for k in range(1, 4):
                to = pl.multiple_of(((second_of[h] + k) % 4) * 16, 16)
                src = s2src.at[li, h, pl.ds(to, 16), :]
                made.append(send(src, s2recv.at[li, h, k - 1], second_at[h](k)))
        return made

    def stage3(li, copies):
        for copy in copies:
            copy.wait_recv()
        for h in range(2):
            mine = pl.multiple_of(second_of[h] * 16, 16)
            part = s2sum[li, h, pl.ds(mine, 16), :]
            for k in range(3):
                part = part + s2recv[li, h, k].astype(F32)
            r16[...] = part
            for zz in range(8):
                for r in range(2):
                    row = zz * 2 + r
                    for lane in range(7):
                        at = (h * 2 + r) * 8 + lane
                        s3sum[li, zz, at : at + 1, :] = r16[
                            row : row + 1, lane * 128 : (lane + 1) * 128
                        ]
        s3src[li] = s3sum[li].astype(BF16)
        made = []
        for k in range(1, 8):
            made.append(send(s3src.at[li, (z + k) % 8], s3recv.at[li, k - 1], at_z(k)))
        return made

    def stage4(li, copies):
        for copy in copies:
            copy.wait_recv()
        part = s3sum[li, z]
        for k in range(7):
            part = part + s3recv[li, k].astype(F32)
        part = part.reshape(4, 8, 128)
        tbuf[li, pl.ds(p * 4, 4)] = part
        return gram_rows(part)

    def shares_spread(li):
        mine = tbuf.at[li, pl.ds(p * 4, 4)]
        return [send(mine, mine, at_eight(k)) for k in range(1, 8)]

    def gram_rows(part):
        lane = lax.broadcasted_iota(jnp.int32, (4, 128), 1)
        tail = part[:, 6, :]
        values = []
        for t in range(3):
            rest = tail if t == 0 else pltpu.roll(tail, 128 - 32 * t, 1)
            rest = jnp.where(lane < 32, rest, 0.0)
            values.append((part[:, 2 * t, :], part[:, 2 * t + 1, :], rest))
        found = {}
        for t in range(3):
            for u in range(t, 3):
                prod = sum(a * b for a, b in zip(values[t], values[u]))
                found[t, u] = found[u, t] = jnp.sum(prod, axis=0, keepdims=True)
        return found

    def own_entries():
        start = (27 * p) // 8
        lane = lax.broadcasted_iota(jnp.int32, (6, 128), 1)
        flat = [jnp.zeros((6, 128), F32) for _ in range(13)]
        for j in range(5):
            row = [tbuf[li, start + j] for li in range(2)]
            pick = lambda s: jnp.concatenate([row[li][s(t)] for li in range(2) for t in range(3)])
            tail = jnp.concatenate(
                [
                    (row[li][6:7] if t == 0 else pltpu.roll(row[li][6:7], 128 - 32 * t, 1))
                    for li in range(2)
                    for t in range(3)
                ]
            )
            tiles = [
                pick(lambda t: slice(2 * t, 2 * t + 1)),
                pick(lambda t: slice(2 * t + 1, 2 * t + 2)),
                jnp.where(lane < 32, tail, 0.0),
            ]
            at, turn = divmod(288 * j, 128)
            for n, tile in enumerate(tiles):
                moved = tile if turn == 0 else pltpu.roll(tile, turn, 1)
                flat[at + n] += jnp.where(lane >= turn, moved, 0.0)
                if turn:
                    flat[at + n + 1] += jnp.where(lane < turn, moved, 0.0)
        width = 13 * 128
        flat = jnp.concatenate(flat, axis=1)
        return pltpu.roll(flat, (width - 36 * ((27 * p) % 8)) % width, 1)

    copy = send(draw.at[1], dpart.at[1], partner)
    reduce2 = stage1(1, D2, [copy])

    blocks_arrived(slope9, blocks)
    for copy in g_copies:
        copy.wait_recv()
    for s in range(9):
        if s == 4:
            continue
        cot = dot(spread_ref[...], three_parts(g9[s]))
        slope = slope9[s].astype(F32)
        for t in range(3):
            d9[t, (8 - s) * C : (9 - s) * C, :] = (cot[t * C : (t + 1) * C, :] * slope).astype(
                BF16
            )
    copies = []
    for t in range(3):
        pbuf[...] = dot(w2t_ref[...], d9[t])
        cot = cotc[t * C : (t + 1) * C, :] + taps_added(pbuf, -D2)
        draw[0, t * C : (t + 1) * C, :] = (cot * slope1[...]).astype(BF16)
        part = pl.ds(t * C, C)
        copies.append(send(draw.at[0, part, :], dpart.at[0, part, :], partner))
    reduce2 = stage2(1, reduce2)
    reduce1 = stage1(0, D1, copies)
    reduce2 = stage3(1, reduce2)
    reduce1 = stage2(0, reduce1)
    found2 = stage4(1, reduce2)
    spread = shares_spread(1)
    reduce1 = stage3(0, reduce1)
    found = (stage4(0, reduce1), found2)
    blank = jnp.zeros((2, 128), F32)
    lane = lax.broadcasted_iota(jnp.int32, (8, 128), 1)
    part = jnp.zeros((8, 128), F32)
    for u in range(3):
        rows = [found[li][t, u] for li in range(2) for t in range(3)] + [blank]
        column = jnp.sum(jnp.concatenate(rows, axis=0), axis=1, keepdims=True)
        part = jnp.where(lane == u, column, part)
    gram_x[p] = part
    copies = [send(gram_x.at[p], gram_x.at[p], at_eight(k)) for k in range(1, 8)]
    spread += shares_spread(0)
    for copy in copies:
        copy.wait_recv()
    part = gram_x[0]
    for j in range(1, 8):
        part = part + gram_x[j]
    gram_z[z] = part
    copies = [send(gram_z.at[z], gram_z.at[z], at_z(k)) for k in range(1, 8)]
    for copy in spread:
        copy.wait_recv()
    entries = own_entries()
    for li in range(2):
        out_ref[li] = entries[3 * li : 3 * li + 3, 0 : out_ref.shape[2]]
    for copy in copies:
        copy.wait_recv()
    part = gram_z[0]
    for j in range(1, 8):
        part = part + gram_z[j]
    unit = core * 2 + yhi
    gram_y[unit] = part
    copies = [send(gram_y.at[unit], gram_y.at[unit], at_unit(k)) for k in range(1, 4)]
    for copy in copies:
        copy.wait_recv()
    part = ((gram_y[0] + gram_y[1]) + (gram_y[2] + gram_y[3])) / NORM
    for li in range(2):
        gram_ref[li] = part[3 * li : 3 * li + 3, 0:3]
    for copy in sent:
        copy.wait_send()


def on_device(
    features,
    conv1_weight,
    conv2_weight,
    fault_head,
    horizon_head,
    salt_query,
    salt_head,
    fault_labels,
    horizon_labels,
    salt_labels,
):
    chans, inline_cells, depth_cells, cross_cells = features.shape
    depth_total = depth_cells * lax.axis_size(TILE)
    scale = 1.0 / math.sqrt(inline_cells * lax.axis_size(INLINE) * depth_total * cross_cells)
    cells = features.transpose(1, 2, 0, 3).reshape(4, C, 128)
    w1 = conv1_weight.transpose(1, 0, 2)
    w2 = conv2_weight.transpose(1, 0, 2)
    blank = jnp.zeros((C, 7), BF16)
    heads = jnp.concatenate(
        [fault_head, horizon_head, salt_query[:, None], salt_head, blank], axis=1
    )
    order = jnp.asarray(row_order(), BF16)

    scratch = [
        pltpu.VMEM((2, 27, C, C), BF16),
        pltpu.VMEM((2, HALF, 9 * C), BF16),
        pltpu.VMEM((3 * C, 9 * C), BF16),
        pltpu.VMEM((3 * C, 9 * C), BF16),
        pltpu.VMEM((3 * C, 9 * C), BF16),
        pltpu.VMEM((3 * C, 48), BF16),
        pltpu.VMEM((16, C, 128), BF16),
        pltpu.VMEM((9 * C, V), BF16),
        pltpu.VMEM((9, C, V), BF16),
        pltpu.VMEM((9, C, V), BF16),
        pltpu.VMEM((9, 16, V), F32),
        pltpu.VMEM((3, 9 * C, V), BF16),
        pltpu.VMEM((C, V), F32),
        pltpu.VMEM((3 * C, V), F32),
        pltpu.VMEM((2, HALF, 2 * V), BF16),
        pltpu.VMEM((2, HALF, V), BF16),
        pltpu.VMEM((2, 3 * C, V), BF16),
        pltpu.VMEM((2, 3 * C, V), BF16),
        pltpu.VMEM((LANES, 2 * V), BF16),
        pltpu.VMEM((3 * C, V), F32),
        pltpu.VMEM((2, HALF, LANES), F32),
        pltpu.VMEM((2, HALF, LANES), BF16),
        pltpu.VMEM((2, 2, 3, 64, LANES), BF16),
        pltpu.VMEM((2, 2, 64, LANES), F32),
        pltpu.VMEM((2, 2, 64, LANES), BF16),
        pltpu.VMEM((2, 2, 3, 16, LANES), BF16),
        pltpu.VMEM((16, LANES), F32),
        pltpu.VMEM((2, 8, 32, 128), F32),
        pltpu.VMEM((2, 8, 32, 128), BF16),
        pltpu.VMEM((2, 7, 32, 128), BF16),
        pltpu.VMEM((2, 32, 8, 128), F32),
        pltpu.VMEM((8, 8, 256), F32),
        pltpu.VMEM((4, 8, 256), F32),
        pltpu.VMEM((8, 8, 128), F32),
        pltpu.VMEM((8, 8, 128), F32),
        pltpu.VMEM((4, 8, 128), F32),
        pltpu.SemaphoreType.DMA((3,)),
        pltpu.SemaphoreType.DMA((136,)),
        pltpu.SemaphoreType.DMA((136,)),
    ]
    whole = pl.BlockSpec(memory_space=pltpu.VMEM)
    hbm = pl.BlockSpec(memory_space=pl.ANY)
    return pl.pallas_call(
        functools.partial(kernel, scale, depth_total * scale),
        out_shape=(
            jax.ShapeDtypeStruct((2, 3, NORM // 256), F32),
            jax.ShapeDtypeStruct((2, 3, 3), F32),
        ),
        in_specs=[whole, hbm, hbm, whole, hbm, whole, whole, whole],
        out_specs=(whole, whole),
        scratch_shapes=scratch,
        compiler_params=pltpu.CompilerParams(
            collective_id=0, has_side_effects=True, vmem_limit_bytes=60 * 1024 * 1024
        ),
    )(cells, w1, w2, heads, order, fault_labels, horizon_labels, salt_labels)


def solution(mesh):
    split = Mesh(
        mesh.devices.reshape(4, 2, 2, 4, 4), ("inline_0", "inline_1", "tile_0", "tile_1", "tile_2")
    )
    return jax.shard_map(
        on_device,
        mesh=split,
        in_specs=(
            P(None, INLINE, TILE, None),
            P(),
            P(),
            P(),
            P(),
            P(),
            P(),
            P(INLINE, TILE, None),
            P(INLINE, TILE, None),
            P(INLINE, None),
        ),
        out_specs=(P(None, None, INLINE_TILE), P()),
        check_vma=False,
    )
```

```python
import functools
import math

import jax
import jax.numpy as jnp
import numpy as np
from jax import lax
from jax.experimental import pallas as pl
from jax.experimental.pallas import tpu as pltpu
from jax.sharding import Mesh
from jax.sharding import PartitionSpec as P

MESH = pl.DeviceIdType.MESH
TILE = ("tile_0", "tile_1", "tile_2")
INLINE = ("inline_0", "inline_1")
INLINE_TILE = INLINE + TILE
D1 = 1
D2 = 2
C = 96
V = 512
CAPPING = 8.0
F32 = jnp.float32
BF16 = jnp.bfloat16
LANES = 896
HALF = 512
NORM = 27 * C * C


def row_order():
    out = np.zeros((2, HALF, 9 * C), np.float32)
    for core in range(2):
        for half in range(2):
            for first in range(4):
                for second in range(4):
                    x, y = (first, second) if half == 0 else (second, first)
                    for z in range(8):
                        for r in range(2):
                            rho = (((y % 2) * 4 + x) * 2 + half) * 2 + r
                            if rho >= 27:
                                continue
                            s, ab = divmod(rho, 9)
                            i = 12 * ((z // 2) * 2 + core) + 3 * ((z % 2) * 2 + y // 2) + s
                            row = (((half * 4 + first) * 4 + second) * 8 + z) * 2 + r
                            out[core, row, ab * C + i] = 1.0
    return out


def shifted(x, k):
    lane = lax.broadcasted_iota(jnp.int32, (x.shape[0], 128), 1) + k
    keep = (lane >= 0) & (lane < 128)
    parts = []
    for j in range(x.shape[1] // 128):
        part = pltpu.roll(x[:, j * 128 : (j + 1) * 128], (-k) % 128, 1)
        parts.append(jnp.where(keep, part, 0.0))
    return jnp.concatenate(parts, axis=1)


def dot(a, b):
    return lax.dot_general(a, b, (((1,), (0,)), ((), ())), preferred_element_type=F32)


def dot_t(a, b):
    return lax.dot_general(a, b, (((1,), (1,)), ((), ())), preferred_element_type=F32)


def capped(value):
    return CAPPING * jnp.tanh(value / CAPPING)


def cap_slope(value):
    squash = jnp.tanh(value / CAPPING)
    return 1.0 - squash * squash


def head_logits(raw, labels, scale):
    expo = [jnp.exp(capped(r)) for r in raw]
    total = functools.reduce(lambda a, b: a + b, expo)
    return [
        (e / total - (labels == n).astype(F32)) * cap_slope(r) * scale
        for n, (e, r) in enumerate(zip(expo, raw))
    ]


def three_parts(g):
    hi = g.astype(BF16).astype(F32)
    rest = g - hi
    mid = rest.astype(BF16).astype(F32)
    parts = [hi, mid, rest - mid, jnp.zeros(g.shape, F32)]
    return jnp.concatenate(parts, axis=0).astype(BF16)


def kernel(
    scale,
    depth_scale,
    feat_ref,
    w1_hbm,
    w2_hbm,
    fault_head,
    horizon_head,
    query_ref,
    salt_head,
    order_hbm,
    fault_ref,
    horizon_ref,
    salt_ref,
    out_ref,
    gram_ref,
    raw_w,
    order_ref,
    w1_ref,
    w2_ref,
    w2t_ref,
    spread_a,
    spread_b,
    fpad,
    f91,
    f92,
    slope9,
    g9a,
    g9b,
    d9,
    slope1,
    cotc,
    amat,
    fsend,
    draw,
    dpart,
    dsh,
    pbuf,
    o32,
    s1src,
    s1recv,
    s2sum,
    s2src,
    s2recv,
    r16,
    s3sum,
    s3src,
    s3recv,
    tbuf,
    pool_x,
    pool_y,
    gram_x,
    gram_z,
    gram_y,
    lsem,
    ssem,
    rsem,
):
    zh, core, zl, y, x = [lax.axis_index(a) for a in INLINE_TILE]
    inline = zh * 2 + core
    tile = zl * 16 + y * 4 + x
    z = zh * 2 + zl
    yhi, ylo = y // 2, y % 2
    p = ylo * 4 + x

    sem_count = [0]
    sent = []

    def send(src, dst, device):
        n = sem_count[0]
        sem_count[0] += 1
        copy = pltpu.make_async_remote_copy(
            src_ref=src,
            dst_ref=dst,
            send_sem=ssem.at[n],
            recv_sem=rsem.at[n],
            device_id=device,
            device_id_type=MESH,
        )
        copy.start()
        sent.append(copy)
        return copy

    def at_grid(dx, dz):
        i = (inline + dx + 8) % 8
        t = (tile + dz + 32) % 32
        return (i // 2, i % 2, t // 16, (t // 4) % 4, t % 4)

    around = [(dx, dz) for dx in (-1, 0, 1) for dz in (-1, 0, 1) if (dx, dz) != (0, 0)]
    halo_to = {d: at_grid(*d) for d in around}

    partner = (zh, 1 - core, zl, y, x)

    def at_x(k):
        return (zh, core, zl, y, (x + k) % 4)

    def at_y(k):
        return (zh, core, zl, (y + k) % 4, x)

    def at_z(k):
        q = (z + k) % 8
        return (q // 2, core, q % 2, y, x)

    def at_eight(k):
        q = (p + k) % 8
        return (zh, core, zl, yhi * 2 + q // 4, q % 4)

    def at_depth(k):
        q = (zl * 2 + yhi + k) % 4
        return (zh, core, q // 2, (q % 2) * 2 + ylo, x)

    def at_unit(k):
        q = (core * 2 + yhi + k) % 4
        return (zh, q // 2, zl, (q % 2) * 2 + ylo, x)

    loads = [
        pltpu.make_async_copy(src, dst, lsem.at[n])
        for n, (src, dst) in enumerate(
            ((w1_hbm, raw_w.at[0]), (w2_hbm, raw_w.at[1]), (order_hbm, order_ref))
        )
    ]
    loads[0].start()

    barrier = pltpu.get_barrier_semaphore()
    greeted = [halo_to[d] for d in around]
    greeted += [at_eight(k) for k in range(1, 8)] + [at_z(k) for k in range(1, 8)]
    greeted += [at_y(2), (zh, core, zl, 3 - y, x)]
    across = (1 - yhi) * 2 + ylo
    greeted += [(zh, core, 1 - zl, across, x), (zh, 1 - core, zl, across, x)]
    for device in greeted:
        pl.semaphore_signal(barrier, inc=1, device_id=device, device_id_type=MESH)

    for cell in range(4):
        fpad[(cell // 2 + 1) * 4 + cell % 2 + 1] = feat_ref[cell]
    for li in range(2):
        s3sum[li] = jnp.zeros(s3sum.shape[1:], F32)
    dsh[864:896, :] = jnp.zeros((32, 1024), BF16)

    eye = (
        lax.broadcasted_iota(jnp.int32, (C, C), 0) == lax.broadcasted_iota(jnp.int32, (C, C), 1)
    ).astype(BF16)

    def transposed_weight(n, out):
        for c in range(3):
            rows = jnp.concatenate([raw_w[n, ab * 3 + c] for ab in range(9)], axis=0)
            out[c * C : (c + 1) * C, :] = dot_t(eye, rows).astype(BF16)

    loads[0].wait()
    loads[2].start()
    loads[1].start()
    transposed_weight(0, w1_ref)
    pl.semaphore_wait(barrier, len(greeted))

    copies = []
    for dx, dz in around:
        for cx in (0, 1) if dx == 0 else ((1,) if dx == 1 else (0,)):
            for cz in (0, 1) if dz == 0 else ((1,) if dz == 1 else (0,)):
                src = (cx + 1) * 4 + cz + 1
                dst = (cx - 2 * dx + 1) * 4 + (cz - 2 * dz + 1)
                copies.append(send(fpad.at[src], fpad.at[dst], halo_to[dx, dz]))
    for copy in copies:
        copy.wait_recv()

    low_x, high_x = inline == 0, inline == 7
    low_z, high_z = tile == 0, tile == 31
    none = jnp.zeros((C, 128), BF16)

    @pl.when(low_x)
    def _():
        for j in range(4):
            fpad[j] = none

    @pl.when(high_x)
    def _():
        for j in range(4):
            fpad[12 + j] = none

    @pl.when(low_z)
    def _():
        for j in range(4):
            fpad[4 * j] = none

    @pl.when(high_z)
    def _():
        for j in range(4):
            fpad[4 * j + 3] = none

    for a in range(3):
        for b in range(3):
            for cell in range(4):
                row = (a * 3 + b) * C
                f91[row : row + C, cell * 128 : (cell + 1) * 128] = fpad[
                    (cell // 2 + a) * 4 + cell % 2 + b
                ]

    def taps_added(pbuf, d):
        return pbuf[C : 2 * C, :] + shifted(pbuf[0:C, :], -d) + shifted(pbuf[2 * C :, :], d)

    pbuf[...] = dot(w1_ref[...], f91[...])
    pre = taps_added(pbuf, D1)
    sig = jax.nn.sigmoid(pre)
    own = jnp.concatenate([feat_ref[cell] for cell in range(4)], axis=1).astype(F32)
    f92[4] = (own + pre * sig).astype(BF16)
    slope1[...] = sig * (1.0 + pre * (1.0 - sig))

    def blocks_around(buffer):
        made = []
        for dx, dz in around:
            slot = (1 - dx) * 3 + (1 - dz)
            made.append(send(buffer.at[4], buffer.at[slot], halo_to[dx, dz]))
        return made

    zs = 2 * core - 1
    zrow = (zs + 1) * 3

    def blocks_sent(buffer):
        own = buffer.at[4]
        far = send(own, buffer.at[(1 - zs) * 3 + 1], at_grid(zs, 0))
        up = send(own, buffer.at[3], halo_to[0, 1])
        down = send(own, buffer.at[5], halo_to[0, -1])
        near = send(own, buffer.at[zrow + 1], partner)
        return far, up, down, near

    def blocks_passed_on(buffer, first):
        far, up, down, near = first
        far.wait_recv()
        passed = [
            send(buffer.at[zrow + 1], buffer.at[zrow], halo_to[0, 1]),
            send(buffer.at[zrow + 1], buffer.at[zrow + 2], halo_to[0, -1]),
        ]
        up.wait_recv()
        passed.append(send(buffer.at[3], buffer.at[zrow], partner))
        down.wait_recv()
        passed.append(send(buffer.at[5], buffer.at[zrow + 2], partner))
        return near, passed

    def blocks_arrived(buffer, second):
        near, passed = second
        near.wait_recv()
        for copy in passed:
            copy.wait_recv()
        for copy in passed:
            copy.wait_send()
        sent[:] = [copy for copy in sent if not any(copy is done for done in passed)]
        clear_outside(buffer)

    def clear_outside(buffer):
        zeros = jnp.zeros(buffer.shape[1:], buffer.dtype)

        @pl.when(low_x)
        def _():
            for j in range(3):
                buffer[j] = zeros

        @pl.when(high_x)
        def _():
            for j in range(3):
                buffer[6 + j] = zeros

        @pl.when(low_z)
        def _():
            for j in range(3):
                buffer[3 * j] = zeros

        @pl.when(high_z)
        def _():
            for j in range(3):
                buffer[3 * j + 2] = zeros

    def rows_exchanged(li, field):
        amat[li, :, 0:V] = dot(order_ref[core], field).astype(BF16)
        fsend[li] = dot(order_ref[1 - core], field).astype(BF16)
        return send(fsend.at[li], amat.at[li, :, V : 2 * V], partner)

    blocks = blocks_sent(f92)
    loads[2].wait()
    row_copy = [rows_exchanged(0, f91[...])]
    blocks = blocks_passed_on(f92, blocks)
    loads[1].wait()
    transposed_weight(1, w2_ref)
    for c in range(3):
        for ab in range(9):
            w2t_ref[c * C : (c + 1) * C, ab * C : (ab + 1) * C] = raw_w[1, ab * 3 + c]
    heads = jnp.concatenate(
        [
            fault_head[...].astype(F32),
            horizon_head[...].astype(F32),
            jnp.zeros((2, C), F32),
            query_ref[...].astype(F32),
            salt_head[...].astype(F32),
            jnp.zeros((5, C), F32),
        ],
        axis=0,
    ).astype(BF16)
    column = dot_t(eye, heads)
    lane = lax.broadcasted_iota(jnp.int32, (C, 16), 1)
    of_task = [jnp.where(lane < 2, column, 0.0), jnp.where((lane >= 2) & (lane < 6), column, 0.0)]
    of_task = jnp.concatenate(of_task, axis=0).astype(BF16)
    row = lax.broadcasted_iota(jnp.int32, (16, 32), 0)
    again = lax.broadcasted_iota(jnp.int32, (16, 32), 1)
    again_a = ((row == again % 8) & (again < 24)).astype(BF16)
    again_b = ((row == again % 8 + 8) & (again < 24)).astype(BF16)
    spread_a[...] = dot(of_task, again_a).astype(BF16)
    spread_b[...] = dot(column.astype(BF16), again_b).astype(BF16)
    blocks_arrived(f92, blocks)

    field9 = f92[...].reshape(9 * C, V)
    pbuf[...] = dot(w2_ref[...], field9)
    pre = taps_added(pbuf, D2)
    sig = jax.nn.sigmoid(pre)
    second = (f92[4].astype(F32) + pre * sig).astype(BF16)
    slope2 = sig * (1.0 + pre * (1.0 - sig))
    slope9[4] = slope2.astype(BF16)

    raw = dot(heads, second)
    rows = [raw[n : n + 1, :] for n in range(11)]
    expo = jnp.exp(capped(rows[8]))

    def depth_sum(r):
        return jnp.concatenate(
            [r[:, 0:128] + r[:, 128:256], r[:, 256:384] + r[:, 384:512]], axis=1
        )

    zero_row = jnp.zeros((1, 256), F32)
    partial = [depth_sum(expo), depth_sum(expo * rows[9]), depth_sum(expo * rows[10])]
    pool_x[p] = jnp.concatenate(partial + [zero_row] * 5, axis=0)
    copies = [send(pool_x.at[p], pool_x.at[p], at_eight(k)) for k in range(1, 8)]
    blocks = blocks_sent(slope9)
    fault = jnp.concatenate([fault_ref[a, b : b + 1, :] for a in (0, 1) for b in (0, 1)], axis=1)
    horizon = jnp.concatenate(
        [horizon_ref[a, b : b + 1, :] for a in (0, 1) for b in (0, 1)], axis=1
    )
    salt = jnp.concatenate([salt_ref[0:1, :], salt_ref[1:2, :]], axis=1)
    logits = head_logits(rows[0:2], fault, scale)
    logits += head_logits(rows[2:6], horizon, scale)
    g = jnp.concatenate(logits + [jnp.zeros((2, V), F32)], axis=0)
    g9a[4] = g
    ga_copies = blocks_around(g9a)

    def own_deltas(tasks, cot):
        for n, t in enumerate(tasks):
            part = cot[n * C : (n + 1) * C, :]
            cotc[t * C : (t + 1) * C, :] = part
            delta = (part * slope2).astype(BF16)
            d9[t, 4 * C : 5 * C, :] = delta
            draw[1, t * C : (t + 1) * C, :] = delta

    def deltas_sent(li, tasks):
        part = pl.ds(tasks[0] * C, len(tasks) * C)
        return send(draw.at[li, part, :], dpart.at[li, part, :], partner)

    own_deltas((0, 1), dot(spread_a[...], three_parts(g)))
    delta_copy = deltas_sent(1, (0, 1))
    row_copy.append(rows_exchanged(1, field9))
    for copy in copies:
        copy.wait_recv()
    pooled = pool_x[0]
    for j in range(1, 8):
        pooled = pooled + pool_x[j]
    quarter = zl * 2 + yhi
    pool_y[quarter] = pooled
    copies = [send(pool_y.at[quarter], pool_y.at[quarter], at_depth(k)) for k in range(1, 4)]
    blocks = blocks_passed_on(slope9, blocks)

    def shifted_deltas(ref, at, d, tasks):
        for t in tasks:
            mid = ref[t * C : (t + 1) * C, :]
            wide = mid.astype(F32)
            low = shifted(wide, d).astype(BF16)
            high = shifted(wide, -d).astype(BF16)
            cols = slice(at, at + V)
            dsh[t * 256 : t * 256 + 96, cols] = low
            dsh[t * 256 + 96 : t * 256 + 192, cols] = mid
            dsh[t * 256 + 192 : t * 256 + 256, cols] = high[0:64, :]
            dsh[768 + 32 * t : 800 + 32 * t, cols] = high[64:96, :]

    def products(li, d, tasks, lanes, delta_copy):
        shifted_deltas(draw.at[li], 0, d, tasks)
        delta_copy.wait_recv()
        shifted_deltas(dpart.at[li], V, d, tasks)
        for h in range(2):
            part = slice(h * 256, (h + 1) * 256)
            prod = dot_t(amat[li, part, :], dsh[lanes, :])
            o32[li, part, lanes] = prod
            s1src[li, part, lanes] = prod.astype(BF16)

    row_copy[1].wait_recv()
    products(1, D2, (0, 1), slice(0, 512), delta_copy)
    for copy in copies:
        copy.wait_recv()
    pooled = (pool_y[0] + pool_y[1]) + (pool_y[2] + pool_y[3])
    total = pooled[0:1, :]
    salt_raw = [pooled[1:2, :] / total, pooled[2:3, :] / total]
    salt_log = head_logits(salt_raw, salt, depth_scale)
    inner = salt_log[0] * salt_raw[0] + salt_log[1] * salt_raw[1]

    def per_cell(r):
        return jnp.concatenate([r[:, 0:128], r[:, 0:128], r[:, 128:256], r[:, 128:256]], axis=1)

    attn = expo / per_cell(total)
    wide = [per_cell(r) for r in salt_log]
    along = wide[0] * rows[9] + wide[1] * rows[10]
    dscore = attn * (along - per_cell(inner)) * cap_slope(rows[8])
    voxel = [dscore, attn * wide[0], attn * wide[1]]
    g = jnp.concatenate(voxel + [jnp.zeros((5, V), F32)], axis=0)
    g9b[4] = g
    gb_copies = blocks_around(g9b)
    own_deltas((2,), dot(spread_b[...], three_parts(g)))
    delta_copy = deltas_sent(1, (2,))

    first_at, first_of = (at_x, at_y), (x, y)
    second_at, second_of = (at_y, at_x), (y, x)

    def stage1(li, lanes):
        made = []
        for h in range(2):
            for k in range(1, 4):
                to = h * 256 + ((first_of[h] + k) % 4) * 64
                src = s1src.at[li, pl.ds(pl.multiple_of(to, 64), 64), lanes]
                made.append(send(src, s1recv.at[li, h, k - 1, :, lanes], first_at[h](k)))
        return made

    def stage2(li, copies):
        for copy in copies:
            copy.wait_recv()
        made = []
        for h in range(2):
            mine = pl.multiple_of(h * 256 + first_of[h] * 64, 64)
            part = o32[li, pl.ds(mine, 64), :]
            for k in range(3):
                part = part + s1recv[li, h, k].astype(F32)
            s2sum[li, h] = part
            s2src[li, h] = part.astype(BF16)
            for k in range(1, 4):
                to = pl.multiple_of(((second_of[h] + k) % 4) * 16, 16)
                src = s2src.at[li, h, pl.ds(to, 16), :]
                made.append(send(src, s2recv.at[li, h, k - 1], second_at[h](k)))
        return made

    def stage3(li, copies):
        for copy in copies:
            copy.wait_recv()
        for h in range(2):
            mine = pl.multiple_of(second_of[h] * 16, 16)
            part = s2sum[li, h, pl.ds(mine, 16), :]
            for k in range(3):
                part = part + s2recv[li, h, k].astype(F32)
            r16[...] = part
            for zz in range(8):
                for r in range(2):
                    row = zz * 2 + r
                    for lane in range(7):
                        at = (h * 2 + r) * 8 + lane
                        s3sum[li, zz, at : at + 1, :] = r16[
                            row : row + 1, lane * 128 : (lane + 1) * 128
                        ]
        s3src[li] = s3sum[li].astype(BF16)
        made = []
        for k in range(1, 8):
            made.append(send(s3src.at[li, (z + k) % 8], s3recv.at[li, k - 1], at_z(k)))
        return made

    def stage4(li, copies):
        for copy in copies:
            copy.wait_recv()
        part = s3sum[li, z]
        for k in range(7):
            part = part + s3recv[li, k].astype(F32)
        part = part.reshape(4, 8, 128)
        tbuf[li, pl.ds(p * 4, 4)] = part
        return gram_rows(part)

    def shares_spread(li):
        mine = tbuf.at[li, pl.ds(p * 4, 4)]
        return [send(mine, mine, at_eight(k)) for k in range(1, 8)]

    def gram_rows(part):
        lane = lax.broadcasted_iota(jnp.int32, (4, 128), 1)
        tail = part[:, 6, :]
        values = []
        for t in range(3):
            rest = tail if t == 0 else pltpu.roll(tail, 128 - 32 * t, 1)
            rest = jnp.where(lane < 32, rest, 0.0)
            values.append((part[:, 2 * t, :], part[:, 2 * t + 1, :], rest))
        found = {}
        for t in range(3):
            for u in range(t, 3):
                prod = sum(a * b for a, b in zip(values[t], values[u]))
                found[t, u] = found[u, t] = jnp.sum(prod, axis=0, keepdims=True)
        return found

    def own_entries():
        start = (27 * p) // 8
        lane = lax.broadcasted_iota(jnp.int32, (6, 128), 1)
        flat = [jnp.zeros((6, 128), F32) for _ in range(13)]
        for j in range(5):
            row = [tbuf[li, start + j] for li in range(2)]
            pick = lambda s: jnp.concatenate([row[li][s(t)] for li in range(2) for t in range(3)])
            tail = jnp.concatenate(
                [
                    (row[li][6:7] if t == 0 else pltpu.roll(row[li][6:7], 128 - 32 * t, 1))
                    for li in range(2)
                    for t in range(3)
                ]
            )
            tiles = [
                pick(lambda t: slice(2 * t, 2 * t + 1)),
                pick(lambda t: slice(2 * t + 1, 2 * t + 2)),
                jnp.where(lane < 32, tail, 0.0),
            ]
            at, turn = divmod(288 * j, 128)
            for n, tile in enumerate(tiles):
                moved = tile if turn == 0 else pltpu.roll(tile, turn, 1)
                flat[at + n] += jnp.where(lane >= turn, moved, 0.0)
                if turn:
                    flat[at + n + 1] += jnp.where(lane < turn, moved, 0.0)
        width = 13 * 128
        flat = jnp.concatenate(flat, axis=1)
        return pltpu.roll(flat, (width - 36 * ((27 * p) % 8)) % width, 1)

    reduce2 = stage1(1, pl.ds(0, 512))
    products(1, D2, (2,), slice(512, LANES), delta_copy)
    reduce2 += stage1(1, pl.ds(512, LANES - 512))

    def first_deltas(tasks, spread, g9):
        for s in range(9):
            if s == 4:
                continue
            cot = dot(spread[...], three_parts(g9[s]))
            slope = slope9[s].astype(F32)
            for n, t in enumerate(tasks):
                delta = (cot[n * C : (n + 1) * C, :] * slope).astype(BF16)
                d9[t, (8 - s) * C : (9 - s) * C, :] = delta
        for t in tasks:
            pbuf[...] = dot(w2t_ref[...], d9[t])
            cot = cotc[t * C : (t + 1) * C, :] + taps_added(pbuf, -D2)
            draw[0, t * C : (t + 1) * C, :] = (cot * slope1[...]).astype(BF16)
        return deltas_sent(0, tasks)

    blocks_arrived(slope9, blocks)
    for copy in ga_copies:
        copy.wait_recv()
    delta_copy = first_deltas((0, 1), spread_a, g9a)
    row_copy[0].wait_recv()
    products(0, D1, (0, 1), slice(0, 512), delta_copy)
    reduce1 = stage1(0, pl.ds(0, 512))
    for copy in gb_copies:
        copy.wait_recv()
    delta_copy = first_deltas((2,), spread_b, g9b)
    reduce2 = stage2(1, reduce2)
    products(0, D1, (2,), slice(512, LANES), delta_copy)
    reduce1 += stage1(0, pl.ds(512, LANES - 512))
    reduce2 = stage3(1, reduce2)
    reduce1 = stage2(0, reduce1)
    found2 = stage4(1, reduce2)
    spread = shares_spread(1)
    reduce1 = stage3(0, reduce1)
    found = (stage4(0, reduce1), found2)
    blank = jnp.zeros((2, 128), F32)
    lane = lax.broadcasted_iota(jnp.int32, (8, 128), 1)
    part = jnp.zeros((8, 128), F32)
    for u in range(3):
        rows = [found[li][t, u] for li in range(2) for t in range(3)] + [blank]
        column = jnp.sum(jnp.concatenate(rows, axis=0), axis=1, keepdims=True)
        part = jnp.where(lane == u, column, part)
    gram_x[p] = part
    copies = [send(gram_x.at[p], gram_x.at[p], at_eight(k)) for k in range(1, 8)]
    spread += shares_spread(0)
    for copy in copies:
        copy.wait_recv()
    part = gram_x[0]
    for j in range(1, 8):
        part = part + gram_x[j]
    gram_z[z] = part
    copies = [send(gram_z.at[z], gram_z.at[z], at_z(k)) for k in range(1, 8)]
    for copy in spread:
        copy.wait_recv()
    entries = own_entries()
    for li in range(2):
        for t in range(3):
            row = 3 * li + t
            out_ref[t, li : li + 1, :] = entries[row : row + 1, 0 : out_ref.shape[2]]
    for copy in copies:
        copy.wait_recv()
    part = gram_z[0]
    for j in range(1, 8):
        part = part + gram_z[j]
    unit = core * 2 + yhi
    gram_y[unit] = part
    copies = [send(gram_y.at[unit], gram_y.at[unit], at_unit(k)) for k in range(1, 4)]
    for copy in copies:
        copy.wait_recv()
    part = ((gram_y[0] + gram_y[1]) + (gram_y[2] + gram_y[3])) / NORM
    for li in range(2):
        for t in range(3):
            row = 3 * li + t
            gram_ref[t, li : li + 1, :] = part[row : row + 1, 0:3]
    for copy in sent:
        copy.wait_send()


def on_device(
    features,
    conv1_weight,
    conv2_weight,
    fault_head,
    horizon_head,
    salt_query,
    salt_head,
    fault_labels,
    horizon_labels,
    salt_labels,
):
    chans, inline_cells, depth_cells, cross_cells = features.shape
    depth_total = depth_cells * lax.axis_size(TILE)
    scale = 1.0 / math.sqrt(inline_cells * lax.axis_size(INLINE) * depth_total * cross_cells)
    cells = features.transpose(1, 2, 0, 3).reshape(4, C, 128)
    w1 = conv1_weight.transpose(1, 0, 2)
    w2 = conv2_weight.transpose(1, 0, 2)
    order = jnp.asarray(row_order(), BF16)

    scratch = [
        pltpu.VMEM((2, 27, C, C), BF16),
        pltpu.VMEM((2, HALF, 9 * C), BF16),
        pltpu.VMEM((3 * C, 9 * C), BF16),
        pltpu.VMEM((3 * C, 9 * C), BF16),
        pltpu.VMEM((3 * C, 9 * C), BF16),
        pltpu.VMEM((2 * C, 32), BF16),
        pltpu.VMEM((C, 32), BF16),
        pltpu.VMEM((16, C, 128), BF16),
        pltpu.VMEM((9 * C, V), BF16),
        pltpu.VMEM((9, C, V), BF16),
        pltpu.VMEM((9, C, V), BF16),
        pltpu.VMEM((9, 8, V), F32),
        pltpu.VMEM((9, 8, V), F32),
        pltpu.VMEM((3, 9 * C, V), BF16),
        pltpu.VMEM((C, V), F32),
        pltpu.VMEM((3 * C, V), F32),
        pltpu.VMEM((2, HALF, 2 * V), BF16),
        pltpu.VMEM((2, HALF, V), BF16),
        pltpu.VMEM((2, 3 * C, V), BF16),
        pltpu.VMEM((2, 3 * C, V), BF16),
        pltpu.VMEM((LANES, 2 * V), BF16),
        pltpu.VMEM((3 * C, V), F32),
        pltpu.VMEM((2, HALF, LANES), F32),
        pltpu.VMEM((2, HALF, LANES), BF16),
        pltpu.VMEM((2, 2, 3, 64, LANES), BF16),
        pltpu.VMEM((2, 2, 64, LANES), F32),
        pltpu.VMEM((2, 2, 64, LANES), BF16),
        pltpu.VMEM((2, 2, 3, 16, LANES), BF16),
        pltpu.VMEM((16, LANES), F32),
        pltpu.VMEM((2, 8, 32, 128), F32),
        pltpu.VMEM((2, 8, 32, 128), BF16),
        pltpu.VMEM((2, 7, 32, 128), BF16),
        pltpu.VMEM((2, 32, 8, 128), F32),
        pltpu.VMEM((8, 8, 256), F32),
        pltpu.VMEM((4, 8, 256), F32),
        pltpu.VMEM((8, 8, 128), F32),
        pltpu.VMEM((8, 8, 128), F32),
        pltpu.VMEM((4, 8, 128), F32),
        pltpu.SemaphoreType.DMA((3,)),
        pltpu.SemaphoreType.DMA((160,)),
        pltpu.SemaphoreType.DMA((160,)),
    ]
    whole = pl.BlockSpec(memory_space=pltpu.VMEM)
    hbm = pl.BlockSpec(memory_space=pl.ANY)
    grads, gram = pl.pallas_call(
        functools.partial(kernel, scale, depth_total * scale),
        out_shape=(
            jax.ShapeDtypeStruct((3, 2, NORM // 256), F32),
            jax.ShapeDtypeStruct((3, 2, 3), F32),
        ),
        in_specs=[whole, hbm, hbm] + [whole] * 4 + [hbm] + [whole] * 3,
        out_specs=(whole, whole),
        scratch_shapes=scratch,
        compiler_params=pltpu.CompilerParams(
            collective_id=0, has_side_effects=True, vmem_limit_bytes=60 * 1024 * 1024
        ),
    )(
        cells,
        w1,
        w2,
        fault_head.T,
        horizon_head.T,
        salt_query[None],
        salt_head.T,
        order,
        fault_labels,
        horizon_labels,
        salt_labels,
    )
    return grads.transpose(1, 0, 2), gram.transpose(1, 0, 2)


def solution(mesh):
    split = Mesh(
        mesh.devices.reshape(4, 2, 2, 4, 4), ("inline_0", "inline_1", "tile_0", "tile_1", "tile_2")
    )
    return jax.shard_map(
        on_device,
        mesh=split,
        in_specs=(
            P(None, INLINE, TILE, None),
            P(),
            P(),
            P(),
            P(),
            P(),
            P(),
            P(INLINE, TILE, None),
            P(INLINE, TILE, None),
            P(INLINE, None),
        ),
        out_specs=(P(None, None, INLINE_TILE), P()),
        check_vma=False,
    )
```

```python
import functools
import math

import jax
import jax.numpy as jnp
import numpy as np
from jax import lax
from jax.experimental import pallas as pl
from jax.experimental.pallas import tpu as pltpu
from jax.sharding import Mesh
from jax.sharding import PartitionSpec as P

MESH = pl.DeviceIdType.MESH
TILE = ("tile_0", "tile_1", "tile_2")
INLINE = ("inline_0", "inline_1")
INLINE_TILE = INLINE + TILE
D1 = 1
D2 = 2
C = 96
V = 512
CAPPING = 8.0
F32 = jnp.float32
BF16 = jnp.bfloat16
LANES = 896
HALF = 512
NORM = 27 * C * C


def row_order():
    out = np.zeros((2, HALF, 9 * C), np.float32)
    for core in range(2):
        for half in range(2):
            for first in range(4):
                for second in range(4):
                    x, y = (first, second) if half == 0 else (second, first)
                    for z in range(8):
                        for r in range(2):
                            rho = (((y % 2) * 4 + x) * 2 + half) * 2 + r
                            if rho >= 27:
                                continue
                            s, ab = divmod(rho, 9)
                            i = 12 * ((z // 2) * 2 + core) + 3 * ((z % 2) * 2 + y // 2) + s
                            row = (((half * 4 + first) * 4 + second) * 8 + z) * 2 + r
                            out[core, row, ab * C + i] = 1.0
    return out


def shifted(x, k):
    lane = lax.broadcasted_iota(jnp.int32, (x.shape[0], 128), 1) + k
    keep = (lane >= 0) & (lane < 128)
    parts = []
    for j in range(x.shape[1] // 128):
        part = pltpu.roll(x[:, j * 128 : (j + 1) * 128], (-k) % 128, 1)
        parts.append(jnp.where(keep, part, 0.0))
    return jnp.concatenate(parts, axis=1)


def dot(a, b):
    return lax.dot_general(a, b, (((1,), (0,)), ((), ())), preferred_element_type=F32)


def dot_t(a, b):
    return lax.dot_general(a, b, (((1,), (1,)), ((), ())), preferred_element_type=F32)


def capped(value):
    return CAPPING * jnp.tanh(value / CAPPING)


def cap_slope(value):
    squash = jnp.tanh(value / CAPPING)
    return 1.0 - squash * squash


def head_logits(raw, labels, scale):
    expo = [jnp.exp(capped(r)) for r in raw]
    total = functools.reduce(lambda a, b: a + b, expo)
    return [
        (e / total - (labels == n).astype(F32)) * cap_slope(r) * scale
        for n, (e, r) in enumerate(zip(expo, raw))
    ]


def three_parts(g):
    hi = g.astype(BF16).astype(F32)
    rest = g - hi
    mid = rest.astype(BF16).astype(F32)
    parts = [hi, mid, rest - mid, jnp.zeros(g.shape, F32)]
    return jnp.concatenate(parts, axis=0).astype(BF16)


def kernel(
    scale,
    depth_scale,
    feat_ref,
    w1_hbm,
    w2_hbm,
    fault_head,
    horizon_head,
    query_ref,
    salt_head,
    order_hbm,
    fault_ref,
    horizon_ref,
    salt_ref,
    out_ref,
    gram_ref,
    raw_w,
    order_ref,
    w1_ref,
    w2_ref,
    w2t_ref,
    spread_a,
    spread_b,
    fpad,
    f91,
    f92,
    slope9,
    g9a,
    g9b,
    d9,
    slope1,
    cotc,
    amat,
    fsend,
    draw,
    dpart,
    dsh,
    pbuf,
    o32,
    s1src,
    s1recv,
    s2sum,
    s2src,
    s2recv,
    r16,
    s3sum,
    s3src,
    s3recv,
    tbuf,
    pool_x,
    pool_y,
    gram_x,
    gram_z,
    gram_y,
    lsem,
    ssem,
    rsem,
):
    zh, core, zl, y, x = [lax.axis_index(a) for a in INLINE_TILE]
    inline = zh * 2 + core
    tile = zl * 16 + y * 4 + x
    z = zh * 2 + zl
    yhi, ylo = y // 2, y % 2
    p = ylo * 4 + x

    sem_count = [0]
    sent = []

    def send(src, dst, device):
        n = sem_count[0]
        sem_count[0] += 1
        copy = pltpu.make_async_remote_copy(
            src_ref=src,
            dst_ref=dst,
            send_sem=ssem.at[n],
            recv_sem=rsem.at[n],
            device_id=device,
            device_id_type=MESH,
        )
        copy.start()
        sent.append(copy)
        return copy

    def at_grid(dx, dz):
        i = (inline + dx + 8) % 8
        t = (tile + dz + 32) % 32
        return (i // 2, i % 2, t // 16, (t // 4) % 4, t % 4)

    around = [(dx, dz) for dx in (-1, 0, 1) for dz in (-1, 0, 1) if (dx, dz) != (0, 0)]
    halo_to = {d: at_grid(*d) for d in around}

    partner = (zh, 1 - core, zl, y, x)

    def at_x(k):
        return (zh, core, zl, y, (x + k) % 4)

    def at_y(k):
        return (zh, core, zl, (y + k) % 4, x)

    def at_z(k):
        q = (z + k) % 8
        return (q // 2, core, q % 2, y, x)

    def at_eight(k):
        q = (p + k) % 8
        return (zh, core, zl, yhi * 2 + q // 4, q % 4)

    def at_depth(k):
        q = (zl * 2 + yhi + k) % 4
        return (zh, core, q // 2, (q % 2) * 2 + ylo, x)

    def at_unit(k):
        q = (core * 2 + yhi + k) % 4
        return (zh, q // 2, zl, (q % 2) * 2 + ylo, x)

    loads = [
        pltpu.make_async_copy(src, dst, lsem.at[n])
        for n, (src, dst) in enumerate(
            ((w1_hbm, raw_w.at[0]), (w2_hbm, raw_w.at[1]), (order_hbm, order_ref))
        )
    ]
    loads[0].start()

    barrier = pltpu.get_barrier_semaphore()
    greeted = [halo_to[d] for d in around]
    greeted += [at_eight(k) for k in range(1, 8)] + [at_z(k) for k in range(1, 8)]
    greeted += [at_y(2), (zh, core, zl, 3 - y, x)]
    across = (1 - yhi) * 2 + ylo
    greeted += [(zh, core, 1 - zl, across, x), (zh, 1 - core, zl, across, x)]
    for device in greeted:
        pl.semaphore_signal(barrier, inc=1, device_id=device, device_id_type=MESH)

    for cell in range(4):
        fpad[(cell // 2 + 1) * 4 + cell % 2 + 1] = feat_ref[cell]
    for li in range(2):
        s3sum[li] = jnp.zeros(s3sum.shape[1:], F32)
    dsh[864:896, :] = jnp.zeros((32, 1024), BF16)

    eye = (
        lax.broadcasted_iota(jnp.int32, (C, C), 0) == lax.broadcasted_iota(jnp.int32, (C, C), 1)
    ).astype(BF16)

    def transposed_weight(n, out):
        for c in range(3):
            rows = jnp.concatenate([raw_w[n, ab * 3 + c] for ab in range(9)], axis=0)
            out[c * C : (c + 1) * C, :] = dot_t(eye, rows).astype(BF16)

    loads[0].wait()
    loads[2].start()
    loads[1].start()
    transposed_weight(0, w1_ref)
    pl.semaphore_wait(barrier, len(greeted))

    copies = []
    for dx, dz in around:
        for cx in (0, 1) if dx == 0 else ((1,) if dx == 1 else (0,)):
            for cz in (0, 1) if dz == 0 else ((1,) if dz == 1 else (0,)):
                src = (cx + 1) * 4 + cz + 1
                dst = (cx - 2 * dx + 1) * 4 + (cz - 2 * dz + 1)
                copies.append(send(fpad.at[src], fpad.at[dst], halo_to[dx, dz]))
    for copy in copies:
        copy.wait_recv()

    low_x, high_x = inline == 0, inline == 7
    low_z, high_z = tile == 0, tile == 31
    none = jnp.zeros((C, 128), BF16)

    @pl.when(low_x)
    def _():
        for j in range(4):
            fpad[j] = none

    @pl.when(high_x)
    def _():
        for j in range(4):
            fpad[12 + j] = none

    @pl.when(low_z)
    def _():
        for j in range(4):
            fpad[4 * j] = none

    @pl.when(high_z)
    def _():
        for j in range(4):
            fpad[4 * j + 3] = none

    for a in range(3):
        for b in range(3):
            for cell in range(4):
                row = (a * 3 + b) * C
                f91[row : row + C, cell * 128 : (cell + 1) * 128] = fpad[
                    (cell // 2 + a) * 4 + cell % 2 + b
                ]

    def taps_added(pbuf, d):
        return pbuf[C : 2 * C, :] + shifted(pbuf[0:C, :], -d) + shifted(pbuf[2 * C :, :], d)

    pbuf[...] = dot(w1_ref[...], f91[...])
    pre = taps_added(pbuf, D1)
    sig = jax.nn.sigmoid(pre)
    own = jnp.concatenate([feat_ref[cell] for cell in range(4)], axis=1).astype(F32)
    f92[4] = (own + pre * sig).astype(BF16)
    slope1[...] = sig * (1.0 + pre * (1.0 - sig))

    def blocks_around(buffer):
        made = []
        for dx, dz in around:
            slot = (1 - dx) * 3 + (1 - dz)
            made.append(send(buffer.at[4], buffer.at[slot], halo_to[dx, dz]))
        return made

    zs = 2 * core - 1
    zrow = (zs + 1) * 3

    def blocks_sent(buffer):
        own = buffer.at[4]
        far = send(own, buffer.at[(1 - zs) * 3 + 1], at_grid(zs, 0))
        up = send(own, buffer.at[3], halo_to[0, 1])
        down = send(own, buffer.at[5], halo_to[0, -1])
        near = send(own, buffer.at[zrow + 1], partner)
        return far, up, down, near

    def blocks_passed_on(buffer, first):
        far, up, down, near = first
        far.wait_recv()
        passed = [
            send(buffer.at[zrow + 1], buffer.at[zrow], halo_to[0, 1]),
            send(buffer.at[zrow + 1], buffer.at[zrow + 2], halo_to[0, -1]),
        ]
        up.wait_recv()
        passed.append(send(buffer.at[3], buffer.at[zrow], partner))
        down.wait_recv()
        passed.append(send(buffer.at[5], buffer.at[zrow + 2], partner))
        return near, passed

    def blocks_arrived(buffer, second):
        near, passed = second
        near.wait_recv()
        for copy in passed:
            copy.wait_recv()
        for copy in passed:
            copy.wait_send()
        sent[:] = [copy for copy in sent if not any(copy is done for done in passed)]
        clear_outside(buffer)

    def clear_outside(buffer):
        zeros = jnp.zeros(buffer.shape[1:], buffer.dtype)

        @pl.when(low_x)
        def _():
            for j in range(3):
                buffer[j] = zeros

        @pl.when(high_x)
        def _():
            for j in range(3):
                buffer[6 + j] = zeros

        @pl.when(low_z)
        def _():
            for j in range(3):
                buffer[3 * j] = zeros

        @pl.when(high_z)
        def _():
            for j in range(3):
                buffer[3 * j + 2] = zeros

    def rows_exchanged(li, field):
        amat[li, :, 0:V] = dot(order_ref[core], field).astype(BF16)
        fsend[li] = dot(order_ref[1 - core], field).astype(BF16)
        return send(fsend.at[li], amat.at[li, :, V : 2 * V], partner)

    blocks = blocks_sent(f92)
    loads[2].wait()
    row_copy = [rows_exchanged(0, f91[...])]
    blocks = blocks_passed_on(f92, blocks)
    loads[1].wait()
    transposed_weight(1, w2_ref)
    for c in range(3):
        for ab in range(9):
            w2t_ref[c * C : (c + 1) * C, ab * C : (ab + 1) * C] = raw_w[1, ab * 3 + c]
    heads = jnp.concatenate(
        [
            fault_head[...].astype(F32),
            horizon_head[...].astype(F32),
            jnp.zeros((2, C), F32),
            query_ref[...].astype(F32),
            salt_head[...].astype(F32),
            jnp.zeros((5, C), F32),
        ],
        axis=0,
    ).astype(BF16)
    column = dot_t(eye, heads)
    lane = lax.broadcasted_iota(jnp.int32, (C, 16), 1)
    of_task = [jnp.where(lane < 2, column, 0.0), jnp.where((lane >= 2) & (lane < 6), column, 0.0)]
    of_task = jnp.concatenate(of_task, axis=0).astype(BF16)
    row = lax.broadcasted_iota(jnp.int32, (16, 32), 0)
    again = lax.broadcasted_iota(jnp.int32, (16, 32), 1)
    again_a = ((row == again % 8) & (again < 24)).astype(BF16)
    again_b = ((row == again % 8 + 8) & (again < 24)).astype(BF16)
    spread_a[...] = dot(of_task, again_a).astype(BF16)
    spread_b[...] = dot(column.astype(BF16), again_b).astype(BF16)
    blocks_arrived(f92, blocks)

    field9 = f92[...].reshape(9 * C, V)
    pbuf[...] = dot(w2_ref[...], field9)
    pre = taps_added(pbuf, D2)
    sig = jax.nn.sigmoid(pre)
    second = (f92[4].astype(F32) + pre * sig).astype(BF16)
    slope2 = sig * (1.0 + pre * (1.0 - sig))
    slope9[4] = slope2.astype(BF16)

    raw = dot(heads, second)
    rows = [raw[n : n + 1, :] for n in range(11)]
    expo = jnp.exp(capped(rows[8]))

    def depth_sum(r):
        return jnp.concatenate(
            [r[:, 0:128] + r[:, 128:256], r[:, 256:384] + r[:, 384:512]], axis=1
        )

    zero_row = jnp.zeros((1, 256), F32)
    partial = [depth_sum(expo), depth_sum(expo * rows[9]), depth_sum(expo * rows[10])]
    pool_x[p] = jnp.concatenate(partial + [zero_row] * 5, axis=0)
    copies = [send(pool_x.at[p], pool_x.at[p], at_eight(k)) for k in range(1, 8)]
    blocks = blocks_sent(slope9)
    fault = jnp.concatenate([fault_ref[a, b : b + 1, :] for a in (0, 1) for b in (0, 1)], axis=1)
    horizon = jnp.concatenate(
        [horizon_ref[a, b : b + 1, :] for a in (0, 1) for b in (0, 1)], axis=1
    )
    salt = jnp.concatenate([salt_ref[0:1, :], salt_ref[1:2, :]], axis=1)
    logits = head_logits(rows[0:2], fault, scale)
    logits += head_logits(rows[2:6], horizon, scale)
    g = jnp.concatenate(logits + [jnp.zeros((2, V), F32)], axis=0)
    g9a[4] = g
    ga_copies = blocks_around(g9a)

    def own_deltas(tasks, cot):
        for n, t in enumerate(tasks):
            part = cot[n * C : (n + 1) * C, :]
            cotc[t * C : (t + 1) * C, :] = part
            delta = (part * slope2).astype(BF16)
            d9[t, 4 * C : 5 * C, :] = delta
            draw[1, t * C : (t + 1) * C, :] = delta

    def deltas_sent(li, tasks):
        part = pl.ds(tasks[0] * C, len(tasks) * C)
        return send(draw.at[li, part, :], dpart.at[li, part, :], partner)

    own_deltas((0, 1), dot(spread_a[...], three_parts(g)))
    delta_copy = deltas_sent(1, (0, 1))
    row_copy.append(rows_exchanged(1, field9))
    for copy in copies:
        copy.wait_recv()
    pooled = pool_x[0]
    for j in range(1, 8):
        pooled = pooled + pool_x[j]
    quarter = zl * 2 + yhi
    pool_y[quarter] = pooled
    copies = [send(pool_y.at[quarter], pool_y.at[quarter], at_depth(k)) for k in range(1, 4)]
    blocks = blocks_passed_on(slope9, blocks)

    def shifted_deltas(ref, at, d, tasks):
        for t in tasks:
            mid = ref[t * C : (t + 1) * C, :]
            wide = mid.astype(F32)
            low = shifted(wide, d).astype(BF16)
            high = shifted(wide, -d).astype(BF16)
            cols = slice(at, at + V)
            dsh[t * 256 : t * 256 + 96, cols] = low
            dsh[t * 256 + 96 : t * 256 + 192, cols] = mid
            dsh[t * 256 + 192 : t * 256 + 256, cols] = high[0:64, :]
            dsh[768 + 32 * t : 800 + 32 * t, cols] = high[64:96, :]

    def products(li, d, tasks, lanes, delta_copy):
        shifted_deltas(draw.at[li], 0, d, tasks)
        delta_copy.wait_recv()
        shifted_deltas(dpart.at[li], V, d, tasks)
        prod = dot_t(amat[li], dsh[lanes, :])
        o32[li, :, lanes] = prod
        s1src[li, :, lanes] = prod.astype(BF16)

    row_copy[1].wait_recv()
    products(1, D2, (0, 1), slice(0, 512), delta_copy)
    for copy in copies:
        copy.wait_recv()
    pooled = (pool_y[0] + pool_y[1]) + (pool_y[2] + pool_y[3])
    total = pooled[0:1, :]
    salt_raw = [pooled[1:2, :] / total, pooled[2:3, :] / total]
    salt_log = head_logits(salt_raw, salt, depth_scale)
    inner = salt_log[0] * salt_raw[0] + salt_log[1] * salt_raw[1]

    def per_cell(r):
        return jnp.concatenate([r[:, 0:128], r[:, 0:128], r[:, 128:256], r[:, 128:256]], axis=1)

    attn = expo / per_cell(total)
    wide = [per_cell(r) for r in salt_log]
    along = wide[0] * rows[9] + wide[1] * rows[10]
    dscore = attn * (along - per_cell(inner)) * cap_slope(rows[8])
    voxel = [dscore, attn * wide[0], attn * wide[1]]
    g = jnp.concatenate(voxel + [jnp.zeros((5, V), F32)], axis=0)
    g9b[4] = g
    gb_copies = blocks_around(g9b)
    own_deltas((2,), dot(spread_b[...], three_parts(g)))
    delta_copy = deltas_sent(1, (2,))

    first_at, first_of = (at_x, at_y), (x, y)
    second_at, second_of = (at_y, at_x), (y, x)

    def stage1(li, lanes):
        made = []
        for h in range(2):
            for k in range(1, 4):
                to = h * 256 + ((first_of[h] + k) % 4) * 64
                src = s1src.at[li, pl.ds(pl.multiple_of(to, 64), 64), lanes]
                made.append(send(src, s1recv.at[li, h, k - 1, :, lanes], first_at[h](k)))
        return made

    def stage2(li, copies):
        for copy in copies:
            copy.wait_recv()
        made = []
        for h in range(2):
            mine = pl.multiple_of(h * 256 + first_of[h] * 64, 64)
            part = o32[li, pl.ds(mine, 64), :]
            for k in range(3):
                part = part + s1recv[li, h, k].astype(F32)
            s2sum[li, h] = part
            s2src[li, h] = part.astype(BF16)
            for k in range(1, 4):
                to = pl.multiple_of(((second_of[h] + k) % 4) * 16, 16)
                src = s2src.at[li, h, pl.ds(to, 16), :]
                made.append(send(src, s2recv.at[li, h, k - 1], second_at[h](k)))
        return made

    def stage3(li, copies):
        for copy in copies:
            copy.wait_recv()
        for h in range(2):
            mine = pl.multiple_of(second_of[h] * 16, 16)
            part = s2sum[li, h, pl.ds(mine, 16), :]
            for k in range(3):
                part = part + s2recv[li, h, k].astype(F32)
            r16[...] = part
            for zz in range(8):
                for r in range(2):
                    row = zz * 2 + r
                    for lane in range(7):
                        at = (h * 2 + r) * 8 + lane
                        s3sum[li, zz, at : at + 1, :] = r16[
                            row : row + 1, lane * 128 : (lane + 1) * 128
                        ]
        s3src[li] = s3sum[li].astype(BF16)
        made = []
        for k in range(1, 8):
            made.append(send(s3src.at[li, (z + k) % 8], s3recv.at[li, k - 1], at_z(k)))
        return made

    def stage4(li, copies):
        for copy in copies:
            copy.wait_recv()
        part = s3sum[li, z]
        for k in range(7):
            part = part + s3recv[li, k].astype(F32)
        part = part.reshape(4, 8, 128)
        tbuf[li, pl.ds(p * 4, 4)] = part
        return gram_rows(part)

    def shares_spread():
        mine = tbuf.at[:, pl.ds(p * 4, 4)]
        return [send(mine, mine, at_eight(k)) for k in range(1, 8)]

    def gram_rows(part):
        lane = lax.broadcasted_iota(jnp.int32, (4, 128), 1)
        tail = part[:, 6, :]
        values = []
        for t in range(3):
            rest = tail if t == 0 else pltpu.roll(tail, 128 - 32 * t, 1)
            rest = jnp.where(lane < 32, rest, 0.0)
            values.append((part[:, 2 * t, :], part[:, 2 * t + 1, :], rest))
        found = {}
        for t in range(3):
            for u in range(t, 3):
                prod = sum(a * b for a, b in zip(values[t], values[u]))
                found[t, u] = found[u, t] = jnp.sum(prod, axis=0, keepdims=True)
        return found

    def own_entries():
        start = (27 * p) // 8
        lane = lax.broadcasted_iota(jnp.int32, (6, 128), 1)
        flat = [jnp.zeros((6, 128), F32) for _ in range(13)]
        for j in range(5):
            row = [tbuf[li, start + j] for li in range(2)]
            pick = lambda s: jnp.concatenate([row[li][s(t)] for li in range(2) for t in range(3)])
            tail = jnp.concatenate(
                [
                    (row[li][6:7] if t == 0 else pltpu.roll(row[li][6:7], 128 - 32 * t, 1))
                    for li in range(2)
                    for t in range(3)
                ]
            )
            tiles = [
                pick(lambda t: slice(2 * t, 2 * t + 1)),
                pick(lambda t: slice(2 * t + 1, 2 * t + 2)),
                jnp.where(lane < 32, tail, 0.0),
            ]
            at, turn = divmod(288 * j, 128)
            for n, tile in enumerate(tiles):
                moved = tile if turn == 0 else pltpu.roll(tile, turn, 1)
                flat[at + n] += jnp.where(lane >= turn, moved, 0.0)
                if turn:
                    flat[at + n + 1] += jnp.where(lane < turn, moved, 0.0)
        width = 13 * 128
        flat = jnp.concatenate(flat, axis=1)
        return pltpu.roll(flat, (width - 36 * ((27 * p) % 8)) % width, 1)

    reduce2 = stage1(1, pl.ds(0, 512))
    products(1, D2, (2,), slice(512, LANES), delta_copy)
    reduce2 += stage1(1, pl.ds(512, LANES - 512))

    def first_deltas(tasks, spread, g9):
        for s in range(9):
            if s == 4:
                continue
            cot = dot(spread[...], three_parts(g9[s]))
            slope = slope9[s].astype(F32)
            for n, t in enumerate(tasks):
                delta = (cot[n * C : (n + 1) * C, :] * slope).astype(BF16)
                d9[t, (8 - s) * C : (9 - s) * C, :] = delta
        for t in tasks:
            pbuf[...] = dot(w2t_ref[...], d9[t])
            cot = cotc[t * C : (t + 1) * C, :] + taps_added(pbuf, -D2)
            draw[0, t * C : (t + 1) * C, :] = (cot * slope1[...]).astype(BF16)
        return deltas_sent(0, tasks)

    blocks_arrived(slope9, blocks)
    for copy in ga_copies:
        copy.wait_recv()
    delta_copy = first_deltas((0, 1), spread_a, g9a)
    row_copy[0].wait_recv()
    products(0, D1, (0, 1), slice(0, 512), delta_copy)
    reduce1 = stage1(0, pl.ds(0, 512))
    for copy in gb_copies:
        copy.wait_recv()
    delta_copy = first_deltas((2,), spread_b, g9b)
    reduce2 = stage2(1, reduce2)
    products(0, D1, (2,), slice(512, LANES), delta_copy)
    reduce1 += stage1(0, pl.ds(512, LANES - 512))
    reduce1 = stage2(0, reduce1)
    reduce2 = stage3(1, reduce2)
    reduce1 = stage3(0, reduce1)
    found2 = stage4(1, reduce2)
    found = (stage4(0, reduce1), found2)
    blank = jnp.zeros((2, 128), F32)
    lane = lax.broadcasted_iota(jnp.int32, (8, 128), 1)
    part = jnp.zeros((8, 128), F32)
    for u in range(3):
        rows = [found[li][t, u] for li in range(2) for t in range(3)] + [blank]
        column = jnp.sum(jnp.concatenate(rows, axis=0), axis=1, keepdims=True)
        part = jnp.where(lane == u, column, part)
    gram_x[p] = part
    copies = [send(gram_x.at[p], gram_x.at[p], at_eight(k)) for k in range(1, 8)]
    spread = shares_spread()
    for copy in copies:
        copy.wait_recv()
    part = gram_x[0]
    for j in range(1, 8):
        part = part + gram_x[j]
    gram_z[z] = part
    copies = [send(gram_z.at[z], gram_z.at[z], at_z(k)) for k in range(1, 8)]
    for copy in spread:
        copy.wait_recv()
    entries = own_entries()
    for li in range(2):
        for t in range(3):
            row = 3 * li + t
            out_ref[t, li : li + 1, :] = entries[row : row + 1, 0 : out_ref.shape[2]]
    for copy in copies:
        copy.wait_recv()
    part = gram_z[0]
    for j in range(1, 8):
        part = part + gram_z[j]
    unit = core * 2 + yhi
    gram_y[unit] = part
    copies = [send(gram_y.at[unit], gram_y.at[unit], at_unit(k)) for k in range(1, 4)]
    for copy in copies:
        copy.wait_recv()
    part = ((gram_y[0] + gram_y[1]) + (gram_y[2] + gram_y[3])) / NORM
    for li in range(2):
        for t in range(3):
            row = 3 * li + t
            gram_ref[t, li : li + 1, :] = part[row : row + 1, 0:3]
    for copy in sent:
        copy.wait_send()


def on_device(
    features,
    conv1_weight,
    conv2_weight,
    fault_head,
    horizon_head,
    salt_query,
    salt_head,
    fault_labels,
    horizon_labels,
    salt_labels,
):
    chans, inline_cells, depth_cells, cross_cells = features.shape
    depth_total = depth_cells * lax.axis_size(TILE)
    scale = 1.0 / math.sqrt(inline_cells * lax.axis_size(INLINE) * depth_total * cross_cells)
    cells = features.transpose(1, 2, 0, 3).reshape(4, C, 128)
    w1 = conv1_weight.transpose(1, 0, 2)
    w2 = conv2_weight.transpose(1, 0, 2)
    order = jnp.asarray(row_order(), BF16)

    scratch = [
        pltpu.VMEM((2, 27, C, C), BF16),
        pltpu.VMEM((2, HALF, 9 * C), BF16),
        pltpu.VMEM((3 * C, 9 * C), BF16),
        pltpu.VMEM((3 * C, 9 * C), BF16),
        pltpu.VMEM((3 * C, 9 * C), BF16),
        pltpu.VMEM((2 * C, 32), BF16),
        pltpu.VMEM((C, 32), BF16),
        pltpu.VMEM((16, C, 128), BF16),
        pltpu.VMEM((9 * C, V), BF16),
        pltpu.VMEM((9, C, V), BF16),
        pltpu.VMEM((9, C, V), BF16),
        pltpu.VMEM((9, 8, V), F32),
        pltpu.VMEM((9, 8, V), F32),
        pltpu.VMEM((3, 9 * C, V), BF16),
        pltpu.VMEM((C, V), F32),
        pltpu.VMEM((3 * C, V), F32),
        pltpu.VMEM((2, HALF, 2 * V), BF16),
        pltpu.VMEM((2, HALF, V), BF16),
        pltpu.VMEM((2, 3 * C, V), BF16),
        pltpu.VMEM((2, 3 * C, V), BF16),
        pltpu.VMEM((LANES, 2 * V), BF16),
        pltpu.VMEM((3 * C, V), F32),
        pltpu.VMEM((2, HALF, LANES), F32),
        pltpu.VMEM((2, HALF, LANES), BF16),
        pltpu.VMEM((2, 2, 3, 64, LANES), BF16),
        pltpu.VMEM((2, 2, 64, LANES), F32),
        pltpu.VMEM((2, 2, 64, LANES), BF16),
        pltpu.VMEM((2, 2, 3, 16, LANES), BF16),
        pltpu.VMEM((16, LANES), F32),
        pltpu.VMEM((2, 8, 32, 128), F32),
        pltpu.VMEM((2, 8, 32, 128), BF16),
        pltpu.VMEM((2, 7, 32, 128), BF16),
        pltpu.VMEM((2, 32, 8, 128), F32),
        pltpu.VMEM((8, 8, 256), F32),
        pltpu.VMEM((4, 8, 256), F32),
        pltpu.VMEM((8, 8, 128), F32),
        pltpu.VMEM((8, 8, 128), F32),
        pltpu.VMEM((4, 8, 128), F32),
        pltpu.SemaphoreType.DMA((3,)),
        pltpu.SemaphoreType.DMA((160,)),
        pltpu.SemaphoreType.DMA((160,)),
    ]
    whole = pl.BlockSpec(memory_space=pltpu.VMEM)
    hbm = pl.BlockSpec(memory_space=pl.ANY)
    in_hbm = lambda a: pltpu.with_memory_space_constraint(a, pltpu.HBM)
    grads, gram = pl.pallas_call(
        functools.partial(kernel, scale, depth_total * scale),
        out_shape=(
            jax.ShapeDtypeStruct((3, 2, NORM // 256), F32),
            jax.ShapeDtypeStruct((3, 2, 3), F32),
        ),
        in_specs=[whole, hbm, hbm] + [whole] * 4 + [hbm] + [whole] * 3,
        out_specs=(whole, whole),
        scratch_shapes=scratch,
        compiler_params=pltpu.CompilerParams(
            collective_id=0, has_side_effects=True, vmem_limit_bytes=50 * 1024 * 1024
        ),
    )(
        cells,
        in_hbm(w1),
        in_hbm(w2),
        in_hbm(fault_head.T),
        in_hbm(horizon_head.T),
        in_hbm(salt_query[None]),
        in_hbm(salt_head.T),
        in_hbm(order),
        in_hbm(fault_labels),
        in_hbm(horizon_labels),
        in_hbm(salt_labels),
    )
    return grads.transpose(1, 0, 2), gram.transpose(1, 0, 2)


def solution(mesh):
    split = Mesh(
        mesh.devices.reshape(4, 2, 2, 4, 4), ("inline_0", "inline_1", "tile_0", "tile_1", "tile_2")
    )
    return jax.shard_map(
        on_device,
        mesh=split,
        in_specs=(
            P(None, INLINE, TILE, None),
            P(),
            P(),
            P(),
            P(),
            P(),
            P(),
            P(INLINE, TILE, None),
            P(INLINE, TILE, None),
            P(INLINE, None),
        ),
        out_specs=(P(None, None, INLINE_TILE), P()),
        check_vma=False,
    )
```

```python
import functools
import math

import jax
import jax.numpy as jnp
import numpy as np
from jax import lax
from jax.experimental import pallas as pl
from jax.experimental.pallas import tpu as pltpu
from jax.sharding import Mesh
from jax.sharding import PartitionSpec as P

MESH = pl.DeviceIdType.MESH
TILE = ("tile_0", "tile_1", "tile_2")
INLINE = ("inline_0", "inline_1")
INLINE_TILE = INLINE + TILE
D1 = 1
D2 = 2
C = 96
V = 512
CAPPING = 8.0
F32 = jnp.float32
BF16 = jnp.bfloat16
LANES = 896
HALF = 512
NORM = 27 * C * C


def row_order():
    out = np.zeros((2, HALF, 9 * C), np.float32)
    for core in range(2):
        for half in range(2):
            for first in range(4):
                for second in range(4):
                    x, y = (first, second) if half == 0 else (second, first)
                    for z in range(8):
                        for r in range(2):
                            rho = (((y % 2) * 4 + x) * 2 + half) * 2 + r
                            if rho >= 27:
                                continue
                            s, ab = divmod(rho, 9)
                            i = 12 * ((z // 2) * 2 + core) + 3 * ((z % 2) * 2 + y // 2) + s
                            row = (((half * 4 + first) * 4 + second) * 8 + z) * 2 + r
                            out[core, row, ab * C + i] = 1.0
    return out


def shifted(x, k):
    lane = lax.broadcasted_iota(jnp.int32, (x.shape[0], 128), 1) + k
    keep = (lane >= 0) & (lane < 128)
    parts = []
    for j in range(x.shape[1] // 128):
        part = pltpu.roll(x[:, j * 128 : (j + 1) * 128], (-k) % 128, 1)
        parts.append(jnp.where(keep, part, 0.0))
    return jnp.concatenate(parts, axis=1)


def dot(a, b):
    return lax.dot_general(a, b, (((1,), (0,)), ((), ())), preferred_element_type=F32)


def dot_t(a, b):
    return lax.dot_general(a, b, (((1,), (1,)), ((), ())), preferred_element_type=F32)


def capped(value):
    return CAPPING * jnp.tanh(value / CAPPING)


def cap_slope(value):
    squash = jnp.tanh(value / CAPPING)
    return 1.0 - squash * squash


def head_logits(raw, labels, scale):
    expo = [jnp.exp(capped(r)) for r in raw]
    total = functools.reduce(lambda a, b: a + b, expo)
    return [
        (e / total - (labels == n).astype(F32)) * cap_slope(r) * scale
        for n, (e, r) in enumerate(zip(expo, raw))
    ]


def three_parts(g):
    hi = g.astype(BF16).astype(F32)
    rest = g - hi
    mid = rest.astype(BF16).astype(F32)
    parts = [hi, mid, rest - mid, jnp.zeros(g.shape, F32)]
    return jnp.concatenate(parts, axis=0).astype(BF16)


def kernel(
    scale,
    depth_scale,
    feat_ref,
    w1_hbm,
    w2_hbm,
    fault_head,
    horizon_head,
    query_ref,
    salt_head,
    order_hbm,
    fault_ref,
    horizon_ref,
    salt_ref,
    out_ref,
    gram_ref,
    raw_w,
    order_ref,
    w1_ref,
    w2_ref,
    w2t_ref,
    spread_a,
    spread_b,
    fpad,
    f91,
    f92,
    slope9,
    g9a,
    g9b,
    d9,
    slope1,
    cotc,
    amat,
    fsend,
    draw,
    dpart,
    dsh,
    pbuf,
    o32,
    s1src,
    s1recv,
    s2sum,
    s2src,
    s2recv,
    r16,
    s3sum,
    s3src,
    s3recv,
    tbuf,
    pool_x,
    pool_y,
    gram_x,
    gram_z,
    gram_y,
    lsem,
    ssem,
    rsem,
):
    zh, core, zl, y, x = [lax.axis_index(a) for a in INLINE_TILE]
    inline = zh * 2 + core
    tile = zl * 16 + y * 4 + x
    z = zh * 2 + zl
    yhi, ylo = y // 2, y % 2
    p = ylo * 4 + x

    sem_count = [0]
    sent = []

    def send(src, dst, device):
        n = sem_count[0]
        sem_count[0] += 1
        copy = pltpu.make_async_remote_copy(
            src_ref=src,
            dst_ref=dst,
            send_sem=ssem.at[n],
            recv_sem=rsem.at[n],
            device_id=device,
            device_id_type=MESH,
        )
        copy.start()
        sent.append(copy)
        return copy

    def sends_done(keep):
        old = sent[: len(sent) - keep]
        for copy in old:
            copy.wait_send()
        del sent[: len(old)]

    def at_grid(dx, dz):
        i = (inline + dx + 8) % 8
        t = (tile + dz + 32) % 32
        return (i // 2, i % 2, t // 16, (t // 4) % 4, t % 4)

    around = [(dx, dz) for dx in (-1, 0, 1) for dz in (-1, 0, 1) if (dx, dz) != (0, 0)]
    halo_to = {d: at_grid(*d) for d in around}

    partner = (zh, 1 - core, zl, y, x)

    def at_x(k):
        return (zh, core, zl, y, (x + k) % 4)

    def at_y(k):
        return (zh, core, zl, (y + k) % 4, x)

    def at_z(k):
        q = (z + k) % 8
        return (q // 2, core, q % 2, y, x)

    def at_eight(k):
        q = (p + k) % 8
        return (zh, core, zl, yhi * 2 + q // 4, q % 4)

    def at_depth(k):
        q = (zl * 2 + yhi + k) % 4
        return (zh, core, q // 2, (q % 2) * 2 + ylo, x)

    def at_unit(k):
        q = (core * 2 + yhi + k) % 4
        return (zh, q // 2, zl, (q % 2) * 2 + ylo, x)

    loads = [
        pltpu.make_async_copy(src, dst, lsem.at[n])
        for n, (src, dst) in enumerate(
            ((w1_hbm, raw_w.at[0]), (w2_hbm, raw_w.at[1]), (order_hbm, order_ref))
        )
    ]
    loads[0].start()

    barrier = pltpu.get_barrier_semaphore()
    greeted = [halo_to[d] for d in around]
    greeted += [at_eight(k) for k in range(1, 8)] + [at_z(k) for k in range(1, 8)]
    greeted += [at_y(2), (zh, core, zl, 3 - y, x)]
    across = (1 - yhi) * 2 + ylo
    greeted += [(zh, core, 1 - zl, across, x), (zh, 1 - core, zl, across, x)]
    for device in greeted:
        pl.semaphore_signal(barrier, inc=1, device_id=device, device_id_type=MESH)

    for cell in range(4):
        fpad[(cell // 2 + 1) * 4 + cell % 2 + 1] = feat_ref[cell]
    for li in range(2):
        s3sum[li] = jnp.zeros(s3sum.shape[1:], F32)
    dsh[864:896, :] = jnp.zeros((32, 1024), BF16)

    eye = (
        lax.broadcasted_iota(jnp.int32, (C, C), 0) == lax.broadcasted_iota(jnp.int32, (C, C), 1)
    ).astype(BF16)

    def transposed_weight(n, out):
        for c in range(3):
            rows = jnp.concatenate([raw_w[n, ab * 3 + c] for ab in range(9)], axis=0)
            out[c * C : (c + 1) * C, :] = dot_t(eye, rows).astype(BF16)

    loads[0].wait()
    loads[2].start()
    loads[1].start()
    transposed_weight(0, w1_ref)
    pl.semaphore_wait(barrier, len(greeted))

    copies = []
    for dx, dz in around:
        for cx in (0, 1) if dx == 0 else ((1,) if dx == 1 else (0,)):
            for cz in (0, 1) if dz == 0 else ((1,) if dz == 1 else (0,)):
                src = (cx + 1) * 4 + cz + 1
                dst = (cx - 2 * dx + 1) * 4 + (cz - 2 * dz + 1)
                copies.append(send(fpad.at[src], fpad.at[dst], halo_to[dx, dz]))
    for copy in copies:
        copy.wait_recv()

    low_x, high_x = inline == 0, inline == 7
    low_z, high_z = tile == 0, tile == 31
    none = jnp.zeros((C, 128), BF16)

    @pl.when(low_x)
    def _():
        for j in range(4):
            fpad[j] = none

    @pl.when(high_x)
    def _():
        for j in range(4):
            fpad[12 + j] = none

    @pl.when(low_z)
    def _():
        for j in range(4):
            fpad[4 * j] = none

    @pl.when(high_z)
    def _():
        for j in range(4):
            fpad[4 * j + 3] = none

    for a in range(3):
        for b in range(3):
            for cell in range(4):
                row = (a * 3 + b) * C
                f91[row : row + C, cell * 128 : (cell + 1) * 128] = fpad[
                    (cell // 2 + a) * 4 + cell % 2 + b
                ]

    def taps_added(pbuf, d):
        return pbuf[C : 2 * C, :] + shifted(pbuf[0:C, :], -d) + shifted(pbuf[2 * C :, :], d)

    pbuf[...] = dot(w1_ref[...], f91[...])
    pre = taps_added(pbuf, D1)
    sig = jax.nn.sigmoid(pre)
    own = jnp.concatenate([feat_ref[cell] for cell in range(4)], axis=1).astype(F32)
    f92[4] = (own + pre * sig).astype(BF16)
    slope1[...] = sig * (1.0 + pre * (1.0 - sig))

    def blocks_around(buffer):
        made = []
        for dx, dz in around:
            slot = (1 - dx) * 3 + (1 - dz)
            made.append(send(buffer.at[4], buffer.at[slot], halo_to[dx, dz]))
        return made

    zs = 2 * core - 1
    zrow = (zs + 1) * 3

    def blocks_sent(buffer):
        own = buffer.at[4]
        far = send(own, buffer.at[(1 - zs) * 3 + 1], at_grid(zs, 0))
        up = send(own, buffer.at[3], halo_to[0, 1])
        down = send(own, buffer.at[5], halo_to[0, -1])
        near = send(own, buffer.at[zrow + 1], partner)
        return far, up, down, near

    def blocks_passed_on(buffer, first):
        far, up, down, near = first
        far.wait_recv()
        passed = [
            send(buffer.at[zrow + 1], buffer.at[zrow], halo_to[0, 1]),
            send(buffer.at[zrow + 1], buffer.at[zrow + 2], halo_to[0, -1]),
        ]
        up.wait_recv()
        passed.append(send(buffer.at[3], buffer.at[zrow], partner))
        down.wait_recv()
        passed.append(send(buffer.at[5], buffer.at[zrow + 2], partner))
        return near, passed

    def blocks_arrived(buffer, second):
        near, passed = second
        near.wait_recv()
        for copy in passed:
            copy.wait_recv()
        for copy in passed:
            copy.wait_send()
        sent[:] = [copy for copy in sent if not any(copy is done for done in passed)]
        clear_outside(buffer)

    def clear_outside(buffer):
        zeros = jnp.zeros(buffer.shape[1:], buffer.dtype)

        @pl.when(low_x)
        def _():
            for j in range(3):
                buffer[j] = zeros

        @pl.when(high_x)
        def _():
            for j in range(3):
                buffer[6 + j] = zeros

        @pl.when(low_z)
        def _():
            for j in range(3):
                buffer[3 * j] = zeros

        @pl.when(high_z)
        def _():
            for j in range(3):
                buffer[3 * j + 2] = zeros

    def rows_exchanged(li, field):
        amat[li, :, 0:V] = dot(order_ref[core], field).astype(BF16)
        fsend[li] = dot(order_ref[1 - core], field).astype(BF16)
        return send(fsend.at[li], amat.at[li, :, V : 2 * V], partner)

    blocks = blocks_sent(f92)
    loads[2].wait()
    row_copy = [rows_exchanged(0, f91[...])]
    blocks = blocks_passed_on(f92, blocks)
    loads[1].wait()
    transposed_weight(1, w2_ref)
    for c in range(3):
        for ab in range(9):
            w2t_ref[c * C : (c + 1) * C, ab * C : (ab + 1) * C] = raw_w[1, ab * 3 + c]
    heads = jnp.concatenate(
        [
            fault_head[...].astype(F32),
            horizon_head[...].astype(F32),
            jnp.zeros((2, C), F32),
            query_ref[...].astype(F32),
            salt_head[...].astype(F32),
            jnp.zeros((5, C), F32),
        ],
        axis=0,
    ).astype(BF16)
    column = dot_t(eye, heads)
    lane = lax.broadcasted_iota(jnp.int32, (C, 16), 1)
    of_task = [jnp.where(lane < 2, column, 0.0), jnp.where((lane >= 2) & (lane < 6), column, 0.0)]
    of_task = jnp.concatenate(of_task, axis=0).astype(BF16)
    row = lax.broadcasted_iota(jnp.int32, (16, 32), 0)
    again = lax.broadcasted_iota(jnp.int32, (16, 32), 1)
    again_a = ((row == again % 8) & (again < 24)).astype(BF16)
    again_b = ((row == again % 8 + 8) & (again < 24)).astype(BF16)
    spread_a[...] = dot(of_task, again_a).astype(BF16)
    spread_b[...] = dot(column.astype(BF16), again_b).astype(BF16)
    blocks_arrived(f92, blocks)

    field9 = f92[...].reshape(9 * C, V)
    pbuf[...] = dot(w2_ref[...], field9)
    pre = taps_added(pbuf, D2)
    sig = jax.nn.sigmoid(pre)
    second = (f92[4].astype(F32) + pre * sig).astype(BF16)
    slope2 = sig * (1.0 + pre * (1.0 - sig))
    slope9[4] = slope2.astype(BF16)

    raw = dot(heads, second)
    rows = [raw[n : n + 1, :] for n in range(11)]
    expo = jnp.exp(capped(rows[8]))

    def depth_sum(r):
        return jnp.concatenate(
            [r[:, 0:128] + r[:, 128:256], r[:, 256:384] + r[:, 384:512]], axis=1
        )

    zero_row = jnp.zeros((1, 256), F32)
    partial = [depth_sum(expo), depth_sum(expo * rows[9]), depth_sum(expo * rows[10])]
    pool_x[p] = jnp.concatenate(partial + [zero_row] * 5, axis=0)
    copies = [send(pool_x.at[p], pool_x.at[p], at_eight(k)) for k in range(1, 8)]
    blocks = blocks_sent(slope9)
    fault = jnp.concatenate([fault_ref[a, b : b + 1, :] for a in (0, 1) for b in (0, 1)], axis=1)
    horizon = jnp.concatenate(
        [horizon_ref[a, b : b + 1, :] for a in (0, 1) for b in (0, 1)], axis=1
    )
    salt = jnp.concatenate([salt_ref[0:1, :], salt_ref[1:2, :]], axis=1)
    logits = head_logits(rows[0:2], fault, scale)
    logits += head_logits(rows[2:6], horizon, scale)
    g = jnp.concatenate(logits + [jnp.zeros((2, V), F32)], axis=0)
    g9a[4] = g
    ga_copies = blocks_around(g9a)

    def own_deltas(tasks, cot):
        for n, t in enumerate(tasks):
            part = cot[n * C : (n + 1) * C, :]
            cotc[t * C : (t + 1) * C, :] = part
            delta = (part * slope2).astype(BF16)
            d9[t, 4 * C : 5 * C, :] = delta
            draw[1, t * C : (t + 1) * C, :] = delta

    def deltas_sent(li, tasks):
        part = pl.ds(tasks[0] * C, len(tasks) * C)
        return send(draw.at[li, part, :], dpart.at[li, part, :], partner)

    own_deltas((0, 1), dot(spread_a[...], three_parts(g)))
    delta_copy = deltas_sent(1, (0, 1))
    row_copy.append(rows_exchanged(1, field9))
    for copy in copies:
        copy.wait_recv()
    pooled = pool_x[0]
    for j in range(1, 8):
        pooled = pooled + pool_x[j]
    quarter = zl * 2 + yhi
    pool_y[quarter] = pooled
    copies = [send(pool_y.at[quarter], pool_y.at[quarter], at_depth(k)) for k in range(1, 4)]
    blocks = blocks_passed_on(slope9, blocks)

    def shifted_deltas(ref, at, d, tasks):
        for t in tasks:
            mid = ref[t * C : (t + 1) * C, :]
            wide = mid.astype(F32)
            low = shifted(wide, d).astype(BF16)
            high = shifted(wide, -d).astype(BF16)
            cols = slice(at, at + V)
            dsh[t * 256 : t * 256 + 96, cols] = low
            dsh[t * 256 + 96 : t * 256 + 192, cols] = mid
            dsh[t * 256 + 192 : t * 256 + 256, cols] = high[0:64, :]
            dsh[768 + 32 * t : 800 + 32 * t, cols] = high[64:96, :]

    def products(li, d, tasks, lanes, delta_copy):
        shifted_deltas(draw.at[li], 0, d, tasks)
        delta_copy.wait_recv()
        shifted_deltas(dpart.at[li], V, d, tasks)
        prod = dot_t(amat[li], dsh[lanes, :])
        o32[li, :, lanes] = prod
        s1src[li, :, lanes] = prod.astype(BF16)

    row_copy[1].wait_recv()
    products(1, D2, (0, 1), slice(0, 512), delta_copy)
    for copy in copies:
        copy.wait_recv()
    pooled = (pool_y[0] + pool_y[1]) + (pool_y[2] + pool_y[3])
    total = pooled[0:1, :]
    salt_raw = [pooled[1:2, :] / total, pooled[2:3, :] / total]
    salt_log = head_logits(salt_raw, salt, depth_scale)
    inner = salt_log[0] * salt_raw[0] + salt_log[1] * salt_raw[1]

    def per_cell(r):
        return jnp.concatenate([r[:, 0:128], r[:, 0:128], r[:, 128:256], r[:, 128:256]], axis=1)

    attn = expo / per_cell(total)
    wide = [per_cell(r) for r in salt_log]
    along = wide[0] * rows[9] + wide[1] * rows[10]
    dscore = attn * (along - per_cell(inner)) * cap_slope(rows[8])
    voxel = [dscore, attn * wide[0], attn * wide[1]]
    g = jnp.concatenate(voxel + [jnp.zeros((5, V), F32)], axis=0)
    g9b[4] = g
    gb_copies = blocks_around(g9b)
    own_deltas((2,), dot(spread_b[...], three_parts(g)))
    delta_copy = deltas_sent(1, (2,))

    first_at, first_of = (at_x, at_y), (x, y)
    second_at, second_of = (at_y, at_x), (y, x)

    def stage1(li, lanes):
        made = []
        for h in range(2):
            for k in range(1, 4):
                to = h * 256 + ((first_of[h] + k) % 4) * 64
                src = s1src.at[li, pl.ds(pl.multiple_of(to, 64), 64), lanes]
                made.append(send(src, s1recv.at[li, h, k - 1, :, lanes], first_at[h](k)))
        return made

    def stage2(li, copies):
        for copy in copies:
            copy.wait_recv()
        made = []
        for h in range(2):
            mine = pl.multiple_of(h * 256 + first_of[h] * 64, 64)
            part = o32[li, pl.ds(mine, 64), :]
            for k in range(3):
                part = part + s1recv[li, h, k].astype(F32)
            s2sum[li, h] = part
            s2src[li, h] = part.astype(BF16)
            for k in range(1, 4):
                to = pl.multiple_of(((second_of[h] + k) % 4) * 16, 16)
                src = s2src.at[li, h, pl.ds(to, 16), :]
                made.append(send(src, s2recv.at[li, h, k - 1], second_at[h](k)))
        return made

    def stage3(li, copies):
        for copy in copies:
            copy.wait_recv()
        for h in range(2):
            mine = pl.multiple_of(second_of[h] * 16, 16)
            part = s2sum[li, h, pl.ds(mine, 16), :]
            for k in range(3):
                part = part + s2recv[li, h, k].astype(F32)
            r16[...] = part
            for zz in range(8):
                for r in range(2):
                    row = zz * 2 + r
                    for lane in range(7):
                        at = (h * 2 + r) * 8 + lane
                        s3sum[li, zz, at : at + 1, :] = r16[
                            row : row + 1, lane * 128 : (lane + 1) * 128
                        ]
        s3src[li] = s3sum[li].astype(BF16)
        made = []
        for k in range(1, 8):
            made.append(send(s3src.at[li, (z + k) % 8], s3recv.at[li, k - 1], at_z(k)))
        return made

    def stage4(li, copies):
        for copy in copies:
            copy.wait_recv()
        part = s3sum[li, z]
        for k in range(7):
            part = part + s3recv[li, k].astype(F32)
        part = part.reshape(4, 8, 128)
        tbuf[li, pl.ds(p * 4, 4)] = part
        return gram_rows(part)

    def shares_spread():
        mine = tbuf.at[:, pl.ds(p * 4, 4)]
        return [send(mine, mine, at_eight(k)) for k in range(1, 8)]

    def gram_rows(part):
        lane = lax.broadcasted_iota(jnp.int32, (4, 128), 1)
        tail = part[:, 6, :]
        values = []
        for t in range(3):
            rest = tail if t == 0 else pltpu.roll(tail, 128 - 32 * t, 1)
            rest = jnp.where(lane < 32, rest, 0.0)
            values.append((part[:, 2 * t, :], part[:, 2 * t + 1, :], rest))
        found = {}
        for t in range(3):
            for u in range(t, 3):
                prod = sum(a * b for a, b in zip(values[t], values[u]))
                found[t, u] = found[u, t] = jnp.sum(prod, axis=0, keepdims=True)
        return found

    def own_entries():
        start = (27 * p) // 8
        lane = lax.broadcasted_iota(jnp.int32, (6, 128), 1)
        flat = [jnp.zeros((6, 128), F32) for _ in range(13)]
        for j in range(5):
            row = [tbuf[li, start + j] for li in range(2)]
            pick = lambda s: jnp.concatenate([row[li][s(t)] for li in range(2) for t in range(3)])
            tail = jnp.concatenate(
                [
                    (row[li][6:7] if t == 0 else pltpu.roll(row[li][6:7], 128 - 32 * t, 1))
                    for li in range(2)
                    for t in range(3)
                ]
            )
            tiles = [
                pick(lambda t: slice(2 * t, 2 * t + 1)),
                pick(lambda t: slice(2 * t + 1, 2 * t + 2)),
                jnp.where(lane < 32, tail, 0.0),
            ]
            at, turn = divmod(288 * j, 128)
            for n, tile in enumerate(tiles):
                moved = tile if turn == 0 else pltpu.roll(tile, turn, 1)
                flat[at + n] += jnp.where(lane >= turn, moved, 0.0)
                if turn:
                    flat[at + n + 1] += jnp.where(lane < turn, moved, 0.0)
        width = 13 * 128
        flat = jnp.concatenate(flat, axis=1)
        return pltpu.roll(flat, (width - 36 * ((27 * p) % 8)) % width, 1)

    reduce2 = stage1(1, pl.ds(0, 512))
    products(1, D2, (2,), slice(512, LANES), delta_copy)
    reduce2 += stage1(1, pl.ds(512, LANES - 512))

    def first_deltas(tasks, spread, g9):
        for s in range(9):
            if s == 4:
                continue
            cot = dot(spread[...], three_parts(g9[s]))
            slope = slope9[s].astype(F32)
            for n, t in enumerate(tasks):
                delta = (cot[n * C : (n + 1) * C, :] * slope).astype(BF16)
                d9[t, (8 - s) * C : (9 - s) * C, :] = delta
        for t in tasks:
            pbuf[...] = dot(w2t_ref[...], d9[t])
            cot = cotc[t * C : (t + 1) * C, :] + taps_added(pbuf, -D2)
            draw[0, t * C : (t + 1) * C, :] = (cot * slope1[...]).astype(BF16)
        return deltas_sent(0, tasks)

    blocks_arrived(slope9, blocks)
    for copy in ga_copies:
        copy.wait_recv()
    delta_copy = first_deltas((0, 1), spread_a, g9a)
    row_copy[0].wait_recv()
    products(0, D1, (0, 1), slice(0, 512), delta_copy)
    reduce1 = stage1(0, pl.ds(0, 512))
    for copy in gb_copies:
        copy.wait_recv()
    delta_copy = first_deltas((2,), spread_b, g9b)
    reduce2 = stage2(1, reduce2)
    products(0, D1, (2,), slice(512, LANES), delta_copy)
    reduce1 += stage1(0, pl.ds(512, LANES - 512))
    sends_done(25)
    reduce1 = stage2(0, reduce1)
    reduce2 = stage3(1, reduce2)
    reduce1 = stage3(0, reduce1)
    found2 = stage4(1, reduce2)
    found = (stage4(0, reduce1), found2)
    blank = jnp.zeros((2, 128), F32)
    lane = lax.broadcasted_iota(jnp.int32, (8, 128), 1)
    part = jnp.zeros((8, 128), F32)
    for u in range(3):
        rows = [found[li][t, u] for li in range(2) for t in range(3)] + [blank]
        column = jnp.sum(jnp.concatenate(rows, axis=0), axis=1, keepdims=True)
        part = jnp.where(lane == u, column, part)
    gram_x[p] = part
    copies = [send(gram_x.at[p], gram_x.at[p], at_eight(k)) for k in range(1, 8)]
    spread = shares_spread()
    sends_done(14)
    for copy in copies:
        copy.wait_recv()
    part = gram_x[0]
    for j in range(1, 8):
        part = part + gram_x[j]
    gram_z[z] = part
    copies = [send(gram_z.at[z], gram_z.at[z], at_z(k)) for k in range(1, 8)]
    for copy in spread:
        copy.wait_recv()
    entries = own_entries()
    for li in range(2):
        for t in range(3):
            row = 3 * li + t
            out_ref[t, li : li + 1, :] = entries[row : row + 1, 0 : out_ref.shape[2]]
    for copy in copies:
        copy.wait_recv()
    part = gram_z[0]
    for j in range(1, 8):
        part = part + gram_z[j]
    unit = core * 2 + yhi
    gram_y[unit] = part
    copies = [send(gram_y.at[unit], gram_y.at[unit], at_unit(k)) for k in range(1, 4)]
    for copy in copies:
        copy.wait_recv()
    part = ((gram_y[0] + gram_y[1]) + (gram_y[2] + gram_y[3])) / NORM
    for li in range(2):
        for t in range(3):
            row = 3 * li + t
            gram_ref[t, li : li + 1, :] = part[row : row + 1, 0:3]
    sends_done(0)


def on_device(
    features,
    conv1_weight,
    conv2_weight,
    fault_head,
    horizon_head,
    salt_query,
    salt_head,
    fault_labels,
    horizon_labels,
    salt_labels,
):
    chans, inline_cells, depth_cells, cross_cells = features.shape
    depth_total = depth_cells * lax.axis_size(TILE)
    scale = 1.0 / math.sqrt(inline_cells * lax.axis_size(INLINE) * depth_total * cross_cells)
    cells = features.transpose(1, 2, 0, 3).reshape(4, C, 128)
    w1 = conv1_weight.transpose(1, 0, 2)
    w2 = conv2_weight.transpose(1, 0, 2)
    order = jnp.asarray(row_order(), BF16)

    scratch = [
        pltpu.VMEM((2, 27, C, C), BF16),
        pltpu.VMEM((2, HALF, 9 * C), BF16),
        pltpu.VMEM((3 * C, 9 * C), BF16),
        pltpu.VMEM((3 * C, 9 * C), BF16),
        pltpu.VMEM((3 * C, 9 * C), BF16),
        pltpu.VMEM((2 * C, 32), BF16),
        pltpu.VMEM((C, 32), BF16),
        pltpu.VMEM((16, C, 128), BF16),
        pltpu.VMEM((9 * C, V), BF16),
        pltpu.VMEM((9, C, V), BF16),
        pltpu.VMEM((9, C, V), BF16),
        pltpu.VMEM((9, 8, V), F32),
        pltpu.VMEM((9, 8, V), F32),
        pltpu.VMEM((3, 9 * C, V), BF16),
        pltpu.VMEM((C, V), F32),
        pltpu.VMEM((3 * C, V), F32),
        pltpu.VMEM((2, HALF, 2 * V), BF16),
        pltpu.VMEM((2, HALF, V), BF16),
        pltpu.VMEM((2, 3 * C, V), BF16),
        pltpu.VMEM((2, 3 * C, V), BF16),
        pltpu.VMEM((LANES, 2 * V), BF16),
        pltpu.VMEM((3 * C, V), F32),
        pltpu.VMEM((2, HALF, LANES), F32),
        pltpu.VMEM((2, HALF, LANES), BF16),
        pltpu.VMEM((2, 2, 3, 64, LANES), BF16),
        pltpu.VMEM((2, 2, 64, LANES), F32),
        pltpu.VMEM((2, 2, 64, LANES), BF16),
        pltpu.VMEM((2, 2, 3, 16, LANES), BF16),
        pltpu.VMEM((16, LANES), F32),
        pltpu.VMEM((2, 8, 32, 128), F32),
        pltpu.VMEM((2, 8, 32, 128), BF16),
        pltpu.VMEM((2, 7, 32, 128), BF16),
        pltpu.VMEM((2, 32, 8, 128), F32),
        pltpu.VMEM((8, 8, 256), F32),
        pltpu.VMEM((4, 8, 256), F32),
        pltpu.VMEM((8, 8, 128), F32),
        pltpu.VMEM((8, 8, 128), F32),
        pltpu.VMEM((4, 8, 128), F32),
        pltpu.SemaphoreType.DMA((3,)),
        pltpu.SemaphoreType.DMA((160,)),
        pltpu.SemaphoreType.DMA((160,)),
    ]
    whole = pl.BlockSpec(memory_space=pltpu.VMEM)
    hbm = pl.BlockSpec(memory_space=pl.ANY)
    in_hbm = lambda a: pltpu.with_memory_space_constraint(a, pltpu.HBM)
    grads, gram = pl.pallas_call(
        functools.partial(kernel, scale, depth_total * scale),
        out_shape=(
            jax.ShapeDtypeStruct((3, 2, NORM // 256), F32),
            jax.ShapeDtypeStruct((3, 2, 3), F32),
        ),
        in_specs=[whole, hbm, hbm] + [whole] * 4 + [hbm] + [whole] * 3,
        out_specs=(whole, whole),
        scratch_shapes=scratch,
        compiler_params=pltpu.CompilerParams(
            collective_id=0, has_side_effects=True, vmem_limit_bytes=50 * 1024 * 1024
        ),
    )(
        cells,
        in_hbm(w1),
        in_hbm(w2),
        in_hbm(fault_head.T),
        in_hbm(horizon_head.T),
        in_hbm(salt_query[None]),
        in_hbm(salt_head.T),
        in_hbm(order),
        in_hbm(fault_labels),
        in_hbm(horizon_labels),
        in_hbm(salt_labels),
    )
    return grads.transpose(1, 0, 2), gram.transpose(1, 0, 2)


def solution(mesh):
    split = Mesh(
        mesh.devices.reshape(4, 2, 2, 4, 4), ("inline_0", "inline_1", "tile_0", "tile_1", "tile_2")
    )
    return jax.shard_map(
        on_device,
        mesh=split,
        in_specs=(
            P(None, INLINE, TILE, None),
            P(),
            P(),
            P(),
            P(),
            P(),
            P(),
            P(INLINE, TILE, None),
            P(INLINE, TILE, None),
            P(INLINE, None),
        ),
        out_specs=(P(None, None, INLINE_TILE), P()),
        check_vma=False,
    )
```
